512 devices in a mesh: row: 16 (over x, y), col: 32 (over z, core).
Axes of the slice: x: 4, y: 4, z: 16, core: 2. Of those that a mesh axis runs over, the one named last changes fastest.
Arguments:
- centroids: float32 [3, 65536], P(None, ('col', 'row')), may hold values from -5 to 5, as said below
- weight: float32 [65536], P(('col', 'row')), may hold values from 0.5 to 2
- basis: float32 [4, 30, 65536], P(None, None, ('col', 'row')), may hold values from -6 to 6
Outputs:
- new_vector: float32 [4, 65536], P(None, ('col', 'row'))
- hessenberg: float32 [4, 31], replicated
The draws below stay inside these ranges and needn't reach their ends.
Inputs may be any that keep to these rules, and one draw needn't show every extreme that they name: `centroids`: panels are numbered in order of increasing first coordinate.
All inputs are finite; a program needn't handle non-finite values.
Results may differ from the reference program's by a relative error of at most 0.0003.
Values sent between devices are 32-bit elements; how exact they have to be, the bound alone decides.
A program may use at most 64 MiB of HBM per device.

```python
import math
import jax
import jax.numpy as jnp
from jax import lax

SYSTEMS = 4
KRYLOV = 30
PANELS = 65536


def draw_centroids(key, part):
    key = jax.random.fold_in(key, 11)
    key_jitter, key_turn = jax.random.split(key, 2)
    position = jnp.arange(PANELS).astype(jnp.float32)
    jitter = jax.random.uniform(key_jitter, (PANELS,), jnp.float32)
    axial = (position + jitter) / PANELS * 2.0 - 1.0
    azimuth = jax.random.uniform(key_turn, (PANELS,), jnp.float32, -math.pi, math.pi)
    length = 4.0
    radius_now = jnp.sqrt(jnp.maximum(1.0 - axial * axial, 0.0)) + 0.05
    coord_x = length * axial
    coord_y = radius_now * jnp.cos(azimuth)
    coord_z = radius_now * jnp.sin(azimuth)
    return jnp.stack([coord_x, coord_y, coord_z]).astype(jnp.float32)


def shard_levels(stream_key, shape, cuts, smallest, largest):
    level = 1.0
    for axis_at, blocks in cuts:
        steps = jax.random.uniform(jax.random.fold_in(jax.random.fold_in(stream_key, 6), axis_at), (blocks,), jnp.float32, smallest / len(cuts), largest / len(cuts))
        level = level * jnp.repeat(jnp.exp(steps), shape[axis_at] // blocks).reshape((-1,) + (1,) * (len(shape) - 1 - axis_at))
    return level


def normal_values(rng, shape, width, reach, cuts=(), held_as=jnp.bfloat16):
    gain = shard_levels(rng, shape, cuts, -0.22, 0.18) if cuts else 1.0
    array = jax.random.normal(rng, shape, jnp.float32) * width * gain
    return jnp.minimum(jnp.maximum(array, -reach), reach).astype(held_as)


def setup_inputs(seed: int = 0) -> dict:
    streams_of = jax.random.split(jax.random.key(seed), 4)
    return {
        "centroids": draw_centroids(jax.random.fold_in(streams_of[3], 71), 0),
        "weight": jnp.clip(jnp.exp(math.log(2.0) - 1.3862944 * jax.random.uniform(streams_of[1], (PANELS,), jnp.float32) ** shard_levels(streams_of[1], (PANELS,), ((0, 512),), -0.2, 0.2)), 0.5, 2.0),
        "basis": normal_values(streams_of[2], (SYSTEMS, KRYLOV, PANELS), 1.0, 6.0, ((2, 512),), jnp.float32),
    }


core_factor = 16.0
epsilon = 1e-06

def tile_product(target, source, weight, vectors, panel_count):
    distance = (target[0][:, None] - source[0][None, :]) ** 2
    distance = distance + (target[1][:, None] - source[1][None, :]) ** 2
    distance = distance + (target[2][:, None] - source[2][None, :]) ** 2
    kernel_tile = weight[None, :] * lax.rsqrt(distance + core_factor * weight[None, :] / panel_count)
    kernel_tile = kernel_tile / jnp.sqrt(jnp.float32(panel_count))
    return jnp.einsum('rc,sc->sr', kernel_tile, vectors, precision=lax.Precision.HIGHEST)

def apply_rows(targets, sources, weight, vectors, panel_count):
    systems = vectors.shape[0]
    row_count = targets.shape[1]
    col_count = sources.shape[1]
    row_width = math.gcd(row_count, 512)
    col_width = math.gcd(col_count, 2048)
    target_blocks = targets.reshape(3, row_count // row_width, row_width).transpose(1, 0, 2)
    source_blocks = sources.reshape(3, col_count // col_width, col_width).transpose(1, 0, 2)
    weight_blocks = weight.reshape(col_count // col_width, col_width)
    vector_blocks = vectors.reshape(systems, col_count // col_width, col_width).transpose(1, 0, 2)

    def row_block(target):

        def advance(running_sum, pieces):
            source, piece_weights, piece_vectors = pieces
            return (running_sum + tile_product(target, source, piece_weights, piece_vectors, panel_count), None)
        start_total = jnp.zeros((systems, row_width), jnp.float32)
        running_sum, _ = lax.scan(advance, start_total, (source_blocks, weight_blocks, vector_blocks))
        return running_sum
    gathered = lax.map(row_block, target_blocks)
    return gathered.transpose(1, 0, 2).reshape(systems, row_count)

def reference(centroids, weight, basis):
    newest = basis[:, KRYLOV - 1, :]
    applied = apply_rows(centroids, centroids, weight, newest, float(PANELS))
    inv_count = 1.0 / PANELS
    highest = lax.Precision.HIGHEST
    first = jnp.einsum('skn,sn->sk', basis, applied, precision=highest) * inv_count
    once = applied - jnp.einsum('sk,skn->sn', first, basis, precision=highest)
    second = jnp.einsum('skn,sn->sk', basis, once, precision=highest) * inv_count
    twice = once - jnp.einsum('sk,skn->sn', second, basis, precision=highest)
    length = jnp.sqrt(lax.optimization_barrier(jnp.sum(twice * twice, axis=1)) * inv_count + epsilon)
    new_vector = twice / length[:, None]
    hessenberg = jnp.concatenate([first + second, length[:, None]], axis=1)
    return (new_vector, hessenberg)
```

```python
import functools

import jax
import jax.numpy as jnp
import numpy as np
from jax import lax
from jax.experimental import pallas as pl
from jax.experimental.pallas import tpu as pltpu
from jax.sharding import PartitionSpec as P

MESH = pl.DeviceIdType.MESH
f32, bf16 = jnp.float32, jnp.bfloat16
HIGHEST = lax.Precision.HIGHEST

SYSTEMS = 4
KRYLOV = 30
SEG = 128
ROWS = 16
COLS = 32
PANELS = SEG * ROWS * COLS
SOURCES = ROWS * SEG
CHUNK = 256
FEATURES = 128
CORE = 16.0 / PANELS
EPSILON = 1e-06


def selections():
    source = np.zeros((FEATURES, 48), np.float32)
    target = np.zeros((FEATURES, 48), np.float32)
    coarse, fine, one = (0, 8), (16, 24), 38

    def products(at, lefts, rights):
        for left in lefts:
            for right in rights:
                for axis in range(3):
                    source[at, left + axis] = 1
                    target[at, right + axis] = -2
                    at += 1
        return at

    def norms(at, pieces):
        for piece in pieces:
            source[at, piece] = target[at, one] = 1
            source[at + 1, one] = target[at + 1, piece] = 1
            at += 2
        return at

    norms(products(0, coarse, coarse), (32, 33, 34))
    at = products(32, coarse, fine)
    at = products(at, fine, coarse + fine)
    norms(at, (35, 36, 37))
    return source, target


def rounded(a):
    return a.astype(bf16).astype(f32)


def pieces_of(points, extra):
    at = lax.broadcasted_iota(jnp.int32, (8, SEG), 0)
    points = jnp.where(at < 3, points, 0.0)
    coarse = jnp.floor(points * 128.0 + 0.5) * (1.0 / 128.0)
    fine = points - coarse
    coarse_high = rounded(coarse)
    fine_high = rounded(fine)
    fine_low = rounded(fine - fine_high)
    norm = jnp.sum(coarse * coarse, axis=0, keepdims=True)
    rest = jnp.sum(2.0 * coarse * fine + fine * fine, axis=0, keepdims=True) + extra
    tail = jnp.where(at == 6, 1.0, 0.0)
    row = 0
    for whole in (norm, rest):
        for _ in range(3):
            piece = rounded(whole)
            tail = jnp.where(at == row, piece, tail)
            whole = whole - piece
            row += 1
    rows = [coarse_high, coarse - coarse_high, fine_high, fine_low, tail, jnp.zeros((8, SEG), f32)]
    return jnp.concatenate(rows, axis=0).astype(bf16)


def contract(a, b, dims, **kw):
    return lax.dot_general(a, b, ((dims[:1], dims[1:]), ((), ())), preferred_element_type=f32, **kw)


def step_kernel(
    centroids, weight, basis, source_sel, target_sel, new_vector, hessenberg,
    src, tgt, feat, vecs, part, landed, bmat, col_buf, row_buf, send_sem, recv_sem,
):
    r, c = lax.axis_index("row"), lax.axis_index("col")
    barrier = pltpu.get_barrier_semaphore()

    @pl.loop(1, ROWS)
    def _(i):
        pl.semaphore_signal(
            barrier, inc=1, device_id=(lax.rem(r + i, ROWS), c), device_id_type=MESH
        )

    @pl.loop(1, COLS)
    def _(i):
        pl.semaphore_signal(
            barrier, inc=1, device_id=(r, lax.rem(c + i, COLS)), device_id_type=MESH
        )

    def to_rows(buf, slot, sem):
        @pl.loop(1, ROWS)
        def _(i):
            pltpu.make_async_remote_copy(
                src_ref=buf.at[slot], dst_ref=buf.at[slot],
                send_sem=send_sem.at[sem], recv_sem=recv_sem.at[sem],
                device_id=(lax.rem(r + i, ROWS), c), device_id_type=MESH,
            ).start()

    def to_cols(buf, slot, sem):
        @pl.loop(1, COLS)
        def _(i):
            pltpu.make_async_remote_copy(
                src_ref=buf.at[slot], dst_ref=buf.at[slot],
                send_sem=send_sem.at[sem], recv_sem=recv_sem.at[sem],
                device_id=(r, lax.rem(c + i, COLS)), device_id_type=MESH,
            ).start()

    def all_but_one(buf, sem):
        view = buf.at[pl.ds(0, buf.shape[0] - 1)]
        pltpu.make_async_copy(view, view, sem).wait()

    src[r, 0:3, :] = centroids[...]
    src[r, 3:4, :] = weight[...]
    for s in range(SYSTEMS):
        src[r, 4 + s : 5 + s, :] = basis[s, KRYLOV - 1 : KRYLOV, :]
    tgt[c, 0:3, :] = centroids[...]
    tgt[c, 3:4, :] = weight[...]
    bmat[...] = jnp.zeros_like(bmat)
    for s in range(SYSTEMS):
        bmat[32 * s : 32 * s + KRYLOV, :] = basis[s]

    pl.semaphore_wait(barrier, ROWS + COLS - 2)
    to_rows(src, r, 0)
    to_cols(tgt, c, 1)

    all_but_one(src, recv_sem.at[0])
    for b in range(ROWS):
        block = src[b]
        pieces = pieces_of(block, block[3:4] * CORE)
        rows = slice(b * SEG, (b + 1) * SEG)
        feat[rows, :] = contract(pieces, source_sel[...], (0, 1)).astype(bf16)
        scaled = block[4:8] * (block[3:4] * (1.0 / PANELS**0.5))
        high = rounded(scaled)
        vecs[:, rows] = jnp.concatenate(
            [high, scaled - high, jnp.zeros((8, SEG), f32)], axis=0
        ).astype(bf16)

    all_but_one(tgt, recv_sem.at[1])
    chips = COLS // 2
    chip = c // 2

    @pl.loop(0, chips)
    def _(i):
        away = chips // 2 - (i + 1) // 2
        other = lax.rem(chip + chips + away * (2 * lax.rem(i, 2) - 1), chips)
        pieces = []
        for core in range(2):
            block = jnp.concatenate([tgt[2 * other + core], jnp.zeros((4, SEG), f32)], axis=0)
            pieces.append(pieces_of(block, 0.0))
        meets = contract(target_sel[...], jnp.concatenate(pieces, axis=1), (1, 0)).astype(bf16)
        total = jnp.zeros((16, CHUNK), f32)
        for b in range(SOURCES // CHUNK):
            rows = slice(b * CHUNK, (b + 1) * CHUNK)
            entry = lax.rsqrt(contract(feat[rows, :], meets, (1, 0)))
            high = entry.astype(bf16)
            low = (entry - high.astype(f32)).astype(bf16)
            total = total + contract(vecs[:, rows], high, (1, 0))
            total = total + contract(vecs[:, rows], low, (1, 0))
        total = total[0:4] + total[4:8]
        for core in range(2):
            to = 2 * other + core
            mine = total[:, core * SEG : (core + 1) * SEG]

            @pl.when(to == c)
            def _():
                landed[c] = mine

            @pl.when(to != c)
            def _():
                part[to] = mine
                pltpu.make_async_remote_copy(
                    src_ref=part.at[to], dst_ref=landed.at[c],
                    send_sem=send_sem.at[2], recv_sem=recv_sem.at[2],
                    device_id=(r, to), device_id_type=MESH,
                ).start()

    all_but_one(landed, recv_sem.at[2])
    applied = jnp.sum(landed[...], axis=0)
    applied = jnp.concatenate([applied, jnp.zeros((4, SEG), f32)], axis=0)

    system = lax.broadcasted_iota(jnp.int32, (8, SEG), 0)
    lane = lax.broadcasted_iota(jnp.int32, (8, SEG), 1)
    own = lane // 32 == system

    def total_over_devices(local, at):
        col = col_buf.at[at]
        col[c] = local
        to_cols(col, c, 3 + 2 * at)
        all_but_one(col, recv_sem.at[3 + 2 * at])
        row = row_buf.at[at]
        row[r] = jnp.sum(col[...], axis=0)
        to_rows(row, r, 4 + 2 * at)
        all_but_one(row, recv_sem.at[4 + 2 * at])
        return jnp.sum(row[...], axis=0)

    def inner(vector):
        every = contract(vector, bmat[...], (1, 1), precision=HIGHEST)
        return jnp.sum(jnp.where(own, every, 0.0), axis=0, keepdims=True) * (1.0 / PANELS)

    def spread(coefficients):
        return jnp.where(own, jnp.broadcast_to(coefficients, (8, SEG)), 0.0)

    def along(coefficients):
        return contract(spread(coefficients), bmat[...], (1, 0), precision=HIGHEST)

    first = total_over_devices(inner(applied), 0)
    once = applied - along(first)
    second = total_over_devices(inner(once), 1)
    twice = once - along(second)
    square = jnp.sum(twice * twice, axis=1, keepdims=True) * (1.0 / PANELS)
    square = jnp.sum(jnp.where(own, jnp.broadcast_to(square, (8, SEG)), 0.0), axis=0, keepdims=True)
    square = total_over_devices(square, 2)
    length = jnp.sqrt(square + EPSILON)
    each = jnp.sum(jnp.where(lane % 32 == 0, spread(length), 0.0), axis=1, keepdims=True)
    new_vector[...] = (twice / jnp.where(system[:, 0:1] < SYSTEMS, each, 1.0))[0:SYSTEMS]
    column = jnp.where(lane[0:1] % 32 == KRYLOV, length, first + second)
    for s in range(SYSTEMS):
        hessenberg[s : s + 1, :] = column[:, 32 * s : 32 * s + KRYLOV + 1]

    all_but_one(src, send_sem.at[0])
    all_but_one(tgt, send_sem.at[1])
    all_but_one(landed, send_sem.at[2])
    for at in range(3):
        all_but_one(col_buf.at[at], send_sem.at[3 + 2 * at])
        all_but_one(row_buf.at[at], send_sem.at[4 + 2 * at])


def per_device(centroids, weight, basis):
    source, target = selections()
    vmem = pl.BlockSpec(memory_space=pltpu.VMEM)
    return pl.pallas_call(
        step_kernel,
        out_shape=(
            jax.ShapeDtypeStruct((SYSTEMS, SEG), f32),
            jax.ShapeDtypeStruct((SYSTEMS, KRYLOV + 1), f32),
        ),
        in_specs=[vmem] * 5,
        out_specs=(vmem, vmem),
        scratch_shapes=[
            pltpu.VMEM((ROWS, 8, SEG), f32),
            pltpu.VMEM((COLS, 4, SEG), f32),
            pltpu.VMEM((SOURCES, FEATURES), bf16),
            pltpu.VMEM((16, SOURCES), bf16),
            pltpu.VMEM((COLS, 4, SEG), f32),
            pltpu.VMEM((COLS, 4, SEG), f32),
            pltpu.VMEM((SEG, SEG), f32),
            pltpu.VMEM((3, COLS, 1, SEG), f32),
            pltpu.VMEM((3, ROWS, 1, SEG), f32),
            pltpu.SemaphoreType.DMA((9,)),
            pltpu.SemaphoreType.DMA((9,)),
        ],
        compiler_params=pltpu.CompilerParams(
            collective_id=0, has_side_effects=True, vmem_limit_bytes=40 * 2**20
        ),
        name="arnoldi_step",
    )(centroids, weight.reshape(1, SEG), basis, jnp.asarray(source, bf16), jnp.asarray(target, bf16))


def solution(mesh):
    placed = (P(None, ("col", "row")), P(("col", "row")), P(None, None, ("col", "row")))
    return jax.shard_map(
        per_device,
        mesh=mesh,
        in_specs=placed,
        out_specs=(P(None, ("col", "row")), P()),
        check_vma=False,
    )
```

```python
import functools

import jax
import jax.numpy as jnp
import numpy as np
from jax import lax
from jax.experimental import pallas as pl
from jax.experimental.pallas import tpu as pltpu
from jax.sharding import PartitionSpec as P

MESH = pl.DeviceIdType.MESH
f32, bf16 = jnp.float32, jnp.bfloat16
HIGHEST = lax.Precision.HIGHEST

SYSTEMS = 4
KRYLOV = 30
SEG = 128
ROWS = 16
COLS = 32
PANELS = SEG * ROWS * COLS
SOURCES = ROWS * SEG
CHUNK = 256
FEATURES = 128
CORE = 16.0 / PANELS
DEPTH = 16
PLANE = 32
NEAR = 8
DEPTH = 16
PLANE = 32
NEAR = 8
EPSILON = 1e-06


def selections():
    source = np.zeros((FEATURES, 48), np.float32)
    target = np.zeros((FEATURES, 48), np.float32)
    coarse, fine, one = (0, 8), (16, 24), 38

    def products(at, lefts, rights):
        for left in lefts:
            for right in rights:
                for axis in range(3):
                    source[at, left + axis] = 1
                    target[at, right + axis] = -2
                    at += 1
        return at

    def norms(at, pieces):
        for piece in pieces:
            source[at, piece] = target[at, one] = 1
            source[at + 1, one] = target[at + 1, piece] = 1
            at += 2
        return at

    norms(products(0, coarse, coarse), (32, 33, 34))
    at = products(32, coarse, fine)
    at = products(at, fine, coarse + fine)
    norms(at, (35, 36, 37))
    return source, target


def rounded(a):
    return a.astype(bf16).astype(f32)


def pieces_of(points, extra):
    at = lax.broadcasted_iota(jnp.int32, (8, SEG), 0)
    points = jnp.where(at < 3, points, 0.0)
    coarse = jnp.floor(points * 128.0 + 0.5) * (1.0 / 128.0)
    fine = points - coarse
    coarse_high = rounded(coarse)
    fine_high = rounded(fine)
    fine_low = rounded(fine - fine_high)
    norm = jnp.sum(coarse * coarse, axis=0, keepdims=True)
    rest = jnp.sum(2.0 * coarse * fine + fine * fine, axis=0, keepdims=True) + extra
    tail = jnp.where(at == 6, 1.0, 0.0)
    row = 0
    for whole in (norm, rest):
        for _ in range(3):
            piece = rounded(whole)
            tail = jnp.where(at == row, piece, tail)
            whole = whole - piece
            row += 1
    rows = [coarse_high, coarse - coarse_high, fine_high, fine_low, tail, jnp.zeros((8, SEG), f32)]
    return jnp.concatenate(rows, axis=0).astype(bf16)


def contract(a, b, dims, **kw):
    return lax.dot_general(a, b, ((dims[:1], dims[1:]), ((), ())), preferred_element_type=f32, **kw)


def two_sum(a,b):
    s=a+b
    t=s-a
    return s,(a-(s-t))+(b-t)
def pair_sum(p,q):
    s,e=two_sum(p[0],q[0])
    e=e+(p[1]+q[1])
    h=s+e
    return h,e-(h-s)
def pair_product(a,b):
    p=a*b
    ah,bh=rounded(a),rounded(b)
    al,bl=a-ah,b-bh
    return p,((ah*bh-p)+ah*bl+al*bh)+al*bl
def fold(parts):
    while len(parts)>1:
        parts=[pair_sum(*parts[i:i+2]) if i+1<len(parts) else parts[i] for i in range(0,len(parts),2)]
    return parts[0]
def down(p):
    m=p[0].shape[0]//8
    p=fold([(p[0][8*i:8*i+8],p[1][8*i:8*i+8]) for i in range(m)])
    for by in (4,2,1):
        p=pair_sum(p,(pltpu.roll(p[0],by,0),pltpu.roll(p[1],by,0)))
    return p[0][0:1],p[1][0:1]
def across(by_row):
    lane=lax.broadcasted_iota(jnp.int32,(32,SEG),1)//32
    out=by_row[0:32]
    for s in range(1,SYSTEMS):
        out=jnp.where(lane==s,by_row[32*s:32*s+32],out)
    return out
def gram(b):
    slices=[]
    rest=b
    for bits in (4,12,20,28):
        q=jnp.floor(rest*2.0**bits+0.5)*2.0**-bits
        rest=rest-q
        slices.append(q.astype(bf16))
    total=None
    for level in range(5):
        pairs=[(i,level-i) for i in range(4) if 0<=level-i<4]
        left=jnp.concatenate([slices[i] for i,_ in pairs],axis=1)
        right=jnp.concatenate([slices[j] for _,j in pairs],axis=1)
        part=across(contract(left,right,(1,1)))
        exact=(part,jnp.zeros_like(part))
        total=exact if total is None else pair_sum(total,exact)
    return total[0]*(1.0/PANELS),total[1]*(1.0/PANELS)
def payload(a,bt):
    lane=lax.broadcasted_iota(jnp.int32,(SEG,SEG),1)%32
    at=jnp.concatenate([jnp.broadcast_to(a[s:s+1],(32,SEG)) for s in range(SYSTEMS)],axis=0).T
    h,l=down(pair_product(at,jnp.where(lane==KRYLOV,at,bt)))
    return h*(1.0 / PANELS),l*(1.0 / PANELS)
def finish(a,p,g,bmat):
    k=lax.broadcasted_iota(jnp.int32,(1,SEG),1)%32
    system=lax.broadcasted_iota(jnp.int32,(8,SEG),0)
    lane=lax.broadcasted_iota(jnp.int32,(8,SEG),1)
    own=lane//32==system
    def times(c):
        column=across(jnp.broadcast_to(c,(SEG,SEG)).T)
        h,l=pair_product(g[0],column)
        return down((h,l+g[1]*column))
    basis_lane=k<KRYLOV
    fh,fl=jnp.where(basis_lane,p[0],0.0),jnp.where(basis_lane,p[1],0.0)
    gf=times(fh)
    second=(fh-gf[0])+(fl-gf[1])
    c=fh+second
    a8=jnp.concatenate([a,jnp.zeros((4,SEG),f32)],axis=0)
    twice=a8-contract(jnp.where(own,jnp.broadcast_to(c,(8,SEG)),0.0),bmat,(1,0),precision=HIGHEST)
    gc=times(c)
    u=pair_sum(gc,(-2.0*fh,-2.0*fl))
    h,l=pair_product(c,u[0])
    l=l+c*u[1]
    square=(jnp.where(k==KRYLOV,p[0],h),jnp.where(k==KRYLOV,p[1],l))
    for by in (1,2,4,8,16):
        square=pair_sum(square,(pltpu.roll(square[0],by,1),pltpu.roll(square[1],by,1)))
    length=jnp.sqrt(jnp.maximum(square[0]+square[1],0.0)+EPSILON)
    each=jnp.sum(jnp.where(own&(lane%32==31),jnp.broadcast_to(length,(8,SEG)),0.0),axis=1,keepdims=True)
    new=(twice/jnp.where(system[:,0:1]<SYSTEMS,each,1.0))[0:SYSTEMS]
    return new,jnp.where(k==KRYLOV,pltpu.roll(length,SEG-1,1),c)


def load_basis(basis,bmat):
    bmat[...]=jnp.zeros_like(bmat)
    for s in range(SYSTEMS):
        bmat[32*s:32*s+KRYLOV,:]=basis[s]
def two_sum(a,b):
    s=a+b
    t=s-a
    return s,(a-(s-t))+(b-t)
def pair_sum(p,q):
    s,e=two_sum(p[0],q[0])
    e=e+(p[1]+q[1])
    h=s+e
    return h,e-(h-s)
def pair_product(a,b):
    p=a*b
    ah,bh=rounded(a),rounded(b)
    al,bl=a-ah,b-bh
    return p,((ah*bh-p)+ah*bl+al*bh)+al*bl
def fold(parts):
    while len(parts)>1:
        parts=[pair_sum(*parts[i:i+2]) if i+1<len(parts) else parts[i] for i in range(0,len(parts),2)]
    return parts[0]
def down(p):
    m=p[0].shape[0]//8
    p=fold([(p[0][8*i:8*i+8],p[1][8*i:8*i+8]) for i in range(m)])
    for by in (4,2,1):
        p=pair_sum(p,(pltpu.roll(p[0],by,0),pltpu.roll(p[1],by,0)))
    return p[0][0:1],p[1][0:1]
def across(by_row):
    lane=lax.broadcasted_iota(jnp.int32,(32,SEG),1)//32
    out=by_row[0:32]
    for s in range(1,SYSTEMS):
        out=jnp.where(lane==s,by_row[32*s:32*s+32],out)
    return out
def gram(b):
    slices=[]
    rest=b
    for bits in (4,12,20,28):
        q=jnp.floor(rest*2.0**bits+0.5)*2.0**-bits
        rest=rest-q
        slices.append(q.astype(bf16))
    total=None
    for level in range(5):
        pairs=[(i,level-i) for i in range(4) if 0<=level-i<4]
        left=jnp.concatenate([slices[i] for i,_ in pairs],axis=1)
        right=jnp.concatenate([slices[j] for _,j in pairs],axis=1)
        part=across(contract(left,right,(1,1)))
        exact=(part,jnp.zeros_like(part))
        total=exact if total is None else pair_sum(total,exact)
    return total[0]*(1.0/PANELS),total[1]*(1.0/PANELS)
def payload(a,bt):
    lane=lax.broadcasted_iota(jnp.int32,(SEG,SEG),1)%32
    at=jnp.concatenate([jnp.broadcast_to(a[s:s+1],(32,SEG)) for s in range(SYSTEMS)],axis=0).T
    h,l=down(pair_product(at,jnp.where(lane==KRYLOV,at,bt)))
    return h*(1.0 / PANELS),l*(1.0 / PANELS)
def finish(a,p,g,bmat):
    k=lax.broadcasted_iota(jnp.int32,(1,SEG),1)%32
    system=lax.broadcasted_iota(jnp.int32,(8,SEG),0)
    lane=lax.broadcasted_iota(jnp.int32,(8,SEG),1)
    own=lane//32==system
    def times(c):
        column=across(jnp.broadcast_to(c,(SEG,SEG)).T)
        h,l=pair_product(g[0],column)
        return down((h,l+g[1]*column))
    basis_lane=k<KRYLOV
    fh,fl=jnp.where(basis_lane,p[0],0.0),jnp.where(basis_lane,p[1],0.0)
    gf=times(fh)
    second=(fh-gf[0])+(fl-gf[1])
    c=fh+second
    a8=jnp.concatenate([a,jnp.zeros((4,SEG),f32)],axis=0)
    twice=a8-contract(jnp.where(own,jnp.broadcast_to(c,(8,SEG)),0.0),bmat,(1,0),precision=HIGHEST)
    gc=times(c)
    u=pair_sum(gc,(-2.0*fh,-2.0*fl))
    h,l=pair_product(c,u[0])
    l=l+c*u[1]
    square=(jnp.where(k==KRYLOV,p[0],h),jnp.where(k==KRYLOV,p[1],l))
    for by in (1,2,4,8,16):
        square=pair_sum(square,(pltpu.roll(square[0],by,1),pltpu.roll(square[1],by,1)))
    length=jnp.sqrt(jnp.maximum(square[0]+square[1],0.0)+EPSILON)
    each=jnp.sum(jnp.where(own&(lane%32==31),jnp.broadcast_to(length,(8,SEG)),0.0),axis=1,keepdims=True)
    new=(twice/jnp.where(system[:,0:1]<SYSTEMS,each,1.0))[0:SYSTEMS]
    return new,jnp.where(k==KRYLOV,pltpu.roll(length,SEG-1,1),c)


def step_kernel(
    centroids, weight, basis, source_sel, target_sel, new_vector, hessenberg,
    src, tgt, feat, meet, vecs, sums, part, landed, bmat, bmat_t, gram_out, gram_in, gram_z, gram_all,
    dots_z, dots_q, send_sem, recv_sem,
):
    r, c = lax.axis_index("row"), lax.axis_index("col")
    z, q = c // 2, 2 * r + lax.rem(c, 2)

    def on_line(i):
        return r, lax.rem(c + 2 * i, 2 * DEPTH)

    def on_plane(to):
        return to // 2, 2 * z + lax.rem(to, 2)

    barrier = pltpu.get_barrier_semaphore()

    @pl.loop(1, DEPTH)
    def _(i):
        pl.semaphore_signal(barrier, inc=1, device_id=on_line(i), device_id_type=MESH)

    @pl.loop(1, PLANE)
    def _(i):
        pl.semaphore_signal(
            barrier, inc=1, device_id=on_plane(lax.rem(q + i, PLANE)), device_id_type=MESH
        )

    def send(piece, place, sem, device):
        pltpu.make_async_remote_copy(
            src_ref=piece, dst_ref=place, send_sem=send_sem.at[sem], recv_sem=recv_sem.at[sem],
            device_id=device, device_id_type=MESH,
        ).start()

    def to_line(buf, sem):
        @pl.loop(1, DEPTH)
        def _(i):
            send(buf.at[z], buf.at[z], sem, on_line(i))

    def to_plane(buf, sem):
        @pl.loop(1, PLANE)
        def _(i):
            send(buf.at[q], buf.at[q], sem, on_plane(lax.rem(q + i, PLANE)))

    def settle(buf, count, sem):
        view = buf.at[pl.ds(0, count)]
        pltpu.make_async_copy(view, view, sem).wait()

    own_slot = 3
    src[own_slot, 0:3, :] = centroids[...]
    src[own_slot, 3:4, :] = weight[...]
    for s in range(SYSTEMS):
        src[own_slot, 4 + s : 5 + s, :] = basis[s, KRYLOV - 1 : KRYLOV, :]
    tgt[q, 0:3, :] = centroids[...]
    tgt[q, 3:4, :] = weight[...]
    load_basis(basis, bmat)
    bmat_t[...] = bmat[...].T
    gram_high, gram_low = gram(bmat[...])
    for k in range(PLANE):
        gram_out[k, 0:1, :] = gram_high[k : k + 1]
        gram_out[k, 1:2, :] = gram_low[k : k + 1]

    pl.semaphore_wait(barrier, DEPTH + PLANE - 2)

    def to_slot(i, sem):
        send(src.at[own_slot], src.at[lax.rem(i + own_slot, DEPTH)], sem, on_line(i))

    @pl.loop(1, 5)
    def _(i):
        to_slot(i, 0)

    @pl.loop(13, DEPTH)
    def _(i):
        to_slot(i, 0)

    to_plane(tgt, 2)

    @pl.loop(5, 13)
    def _(i):
        to_slot(i, 1)

    gram_in[q] = gram_out[q]

    @pl.loop(1, PLANE)
    def _(i):
        to = lax.rem(q + i, PLANE)
        send(gram_out.at[to], gram_in.at[q], 3, on_plane(to))

    def prepare(slots):
        for b in slots:
            block = src[b]
            pieces = pieces_of(block, block[3:4] * CORE)
            rows = slice(b * SEG, (b + 1) * SEG)
            feat[rows, :] = contract(pieces, source_sel[...], (0, 1)).astype(bf16)
            scaled = block[4:8] * (block[3:4] * (1.0 / PANELS**0.5))
            high = rounded(scaled)
            vecs[:, rows] = jnp.concatenate(
                [high, scaled - high, jnp.zeros((8, SEG), f32)], axis=0
            ).astype(bf16)

    def operate(meets, total, slots):
        for b in range(slots[0] // 2, slots[1] // 2):
            rows = slice(b * CHUNK, (b + 1) * CHUNK)
            entry = lax.rsqrt(contract(feat[rows, :], meets, (1, 0)))
            high = entry.astype(bf16)
            low = (entry - high.astype(f32)).astype(bf16)
            total = total + contract(vecs[:, rows], high, (1, 0))
            total = total + contract(vecs[:, rows], low, (1, 0))
        return total

    settle(src, NEAR - 1, recv_sem.at[0])
    prepare(range(NEAR))
    settle(tgt, PLANE - 1, recv_sem.at[2])

    @pl.loop(0, ROWS)
    def _(i):
        pieces = []
        for core in range(2):
            block = jnp.concatenate([tgt[2 * i + core], jnp.zeros((4, SEG), f32)], axis=0)
            pieces.append(pieces_of(block, 0.0))
        meets = contract(target_sel[...], jnp.concatenate(pieces, axis=1), (1, 0)).astype(bf16)
        meet[i] = meets
        sums[i] = operate(meets, jnp.zeros((16, CHUNK), f32), (0, NEAR))

    def collect(buf, count):
        return fold([(buf[i, 0:1, :], buf[i, 1:2, :]) for i in range(count)])

    settle(gram_in, PLANE - 1, recv_sem.at[3])
    high, low = collect(gram_in, PLANE)
    gram_z[z, 0:1, :] = high
    gram_z[z, 1:2, :] = low
    to_line(gram_z, 4)

    settle(src, DEPTH - NEAR, recv_sem.at[1])
    prepare(range(NEAR, DEPTH))

    def away(i):
        return lax.rem(2 + i * (i + 1) // 2, 4)

    @pl.loop(0, ROWS)
    def _(i):
        x = lax.rem(r // 4 + away(i // 4), 4)
        y = lax.rem(lax.rem(r, 4) + away(lax.rem(i, 4)), 4)
        other = 4 * x + y
        total = operate(meet[other], sums[other], (NEAR, DEPTH))
        total = total[0:4] + total[4:8]
        for core in range(2):
            to = 2 * other + core
            mine = total[:, core * SEG : (core + 1) * SEG]

            @pl.when(to == q)
            def _():
                landed[q] = mine

            @pl.when(to != q)
            def _():
                part[to] = mine
                send(part.at[to], landed.at[q], 6, on_plane(to))

    settle(gram_z, DEPTH - 1, recv_sem.at[4])
    high, low = collect(gram_z, DEPTH)
    gram_all[q, 0:1, :] = high
    gram_all[q, 1:2, :] = low
    to_plane(gram_all, 5)

    settle(landed, PLANE - 1, recv_sem.at[6])
    applied = jnp.sum(landed[...], axis=0)

    high, low = payload(applied, bmat_t[...])
    dots_z[z, 0:1, :] = high
    dots_z[z, 1:2, :] = low
    to_line(dots_z, 7)
    settle(dots_z, DEPTH - 1, recv_sem.at[7])
    high, low = collect(dots_z, DEPTH)
    dots_q[q, 0:1, :] = high
    dots_q[q, 1:2, :] = low
    to_plane(dots_q, 8)
    settle(gram_all, PLANE - 1, recv_sem.at[5])
    gram_high = jnp.concatenate([gram_all[k, 0:1, :] for k in range(PLANE)], axis=0)
    gram_low = jnp.concatenate([gram_all[k, 1:2, :] for k in range(PLANE)], axis=0)
    settle(dots_q, PLANE - 1, recv_sem.at[8])
    vector, column = finish(applied, collect(dots_q, PLANE), (gram_high, gram_low), bmat[...])
    new_vector[...] = vector
    for s in range(SYSTEMS):
        hessenberg[s : s + 1, :] = column[:, 32 * s : 32 * s + KRYLOV + 1]

    settle(src, NEAR - 1, send_sem.at[0])
    settle(src, DEPTH - NEAR, send_sem.at[1])
    settle(tgt, PLANE - 1, send_sem.at[2])
    settle(gram_in, PLANE - 1, send_sem.at[3])
    settle(gram_z, DEPTH - 1, send_sem.at[4])
    settle(gram_all, PLANE - 1, send_sem.at[5])
    settle(landed, PLANE - 1, send_sem.at[6])
    settle(dots_z, DEPTH - 1, send_sem.at[7])
    settle(dots_q, PLANE - 1, send_sem.at[8])

def per_device(centroids, weight, basis):
    source, target = selections()
    vmem = pl.BlockSpec(memory_space=pltpu.VMEM)
    return pl.pallas_call(
        step_kernel,
        out_shape=(
            jax.ShapeDtypeStruct((SYSTEMS, SEG), f32),
            jax.ShapeDtypeStruct((SYSTEMS, KRYLOV + 1), f32),
        ),
        in_specs=[vmem] * 5,
        out_specs=(vmem, vmem),
        scratch_shapes=[
            pltpu.VMEM((DEPTH, 8, SEG), f32),
            pltpu.VMEM((PLANE, 4, SEG), f32),
            pltpu.VMEM((SOURCES, FEATURES), bf16),
            pltpu.VMEM((ROWS, FEATURES, CHUNK), bf16),
            pltpu.VMEM((16, SOURCES), bf16),
            pltpu.VMEM((ROWS, 16, CHUNK), f32),
            pltpu.VMEM((PLANE, 4, SEG), f32),
            pltpu.VMEM((PLANE, 4, SEG), f32),
            pltpu.VMEM((SEG, SEG), f32),
            pltpu.VMEM((SEG, SEG), f32),
            pltpu.VMEM((PLANE, 2, SEG), f32),
            pltpu.VMEM((PLANE, 2, SEG), f32),
            pltpu.VMEM((DEPTH, 2, SEG), f32),
            pltpu.VMEM((PLANE, 2, SEG), f32),
            pltpu.VMEM((DEPTH, 2, SEG), f32),
            pltpu.VMEM((PLANE, 2, SEG), f32),
            pltpu.SemaphoreType.DMA((9,)),
            pltpu.SemaphoreType.DMA((9,)),
        ],
        compiler_params=pltpu.CompilerParams(
            collective_id=0, has_side_effects=True, vmem_limit_bytes=40 * 2**20
        ),
        name="arnoldi_step",
    )(centroids, weight.reshape(1, SEG), basis, jnp.asarray(source, bf16), jnp.asarray(target, bf16))


def solution(mesh):
    placed = (P(None, ("col", "row")), P(("col", "row")), P(None, None, ("col", "row")))
    return jax.shard_map(
        per_device,
        mesh=mesh,
        in_specs=placed,
        out_specs=(P(None, ("col", "row")), P()),
        check_vma=False,
    )
```

```python
import functools

import jax
import jax.numpy as jnp
import numpy as np
from jax import lax
from jax.experimental import pallas as pl
from jax.experimental.pallas import tpu as pltpu
from jax.sharding import PartitionSpec as P

MESH = pl.DeviceIdType.MESH
f32, bf16 = jnp.float32, jnp.bfloat16
HIGHEST = lax.Precision.HIGHEST

SYSTEMS = 4
KRYLOV = 30
SEG = 128
ROWS = 16
COLS = 32
PANELS = SEG * ROWS * COLS
SOURCES = ROWS * SEG
CHUNK = 256
FEATURES = 128
CORE = 16.0 / PANELS
DEPTH = 16
PLANE = 32
NEAR = 8
REACH = 4
OUTWARD = (
    ((2, 2), (3, 2), (3, 3), (3, 0)),
    ((2, 1), (1, 1), (2, 0), (0, 1)),
    ((2, 3), (1, 3), (0, 2), (0, 3)),
    ((1, 2), (3, 1), (1, 0), (0, 0)),
)
EPSILON = 1e-06


def selections():
    source = np.zeros((FEATURES, 48), np.float32)
    target = np.zeros((FEATURES, 48), np.float32)
    coarse, fine, one = (0, 8), (16, 24), 38

    def products(at, lefts, rights):
        for left in lefts:
            for right in rights:
                for axis in range(3):
                    source[at, left + axis] = 1
                    target[at, right + axis] = -2
                    at += 1
        return at

    def norms(at, pieces):
        for piece in pieces:
            source[at, piece] = target[at, one] = 1
            source[at + 1, one] = target[at + 1, piece] = 1
            at += 2
        return at

    norms(products(0, coarse, coarse), (32, 33, 34))
    at = products(32, coarse, fine)
    at = products(at, fine, coarse + fine)
    norms(at, (35, 36, 37))
    return source, target


def rounded(a):
    return a.astype(bf16).astype(f32)


def pieces_of(points, extra):
    at = lax.broadcasted_iota(jnp.int32, (8, SEG), 0)
    points = jnp.where(at < 3, points, 0.0)
    coarse = jnp.floor(points * 128.0 + 0.5) * (1.0 / 128.0)
    fine = points - coarse
    coarse_high = rounded(coarse)
    fine_high = rounded(fine)
    fine_low = rounded(fine - fine_high)
    norm = jnp.sum(coarse * coarse, axis=0, keepdims=True)
    rest = jnp.sum(2.0 * coarse * fine + fine * fine, axis=0, keepdims=True) + extra
    tail = jnp.where(at == 6, 1.0, 0.0)
    row = 0
    for whole in (norm, rest):
        for _ in range(3):
            piece = rounded(whole)
            tail = jnp.where(at == row, piece, tail)
            whole = whole - piece
            row += 1
    rows = [coarse_high, coarse - coarse_high, fine_high, fine_low, tail, jnp.zeros((8, SEG), f32)]
    return jnp.concatenate(rows, axis=0).astype(bf16)


def contract(a, b, dims, **kw):
    return lax.dot_general(a, b, ((dims[:1], dims[1:]), ((), ())), preferred_element_type=f32, **kw)


def load_basis(basis,bmat):
    bmat[...]=jnp.zeros_like(bmat)
    for s in range(SYSTEMS):
        bmat[32*s:32*s+KRYLOV,:]=basis[s]
def two_sum(a,b):
    s=a+b
    t=s-a
    return s,(a-(s-t))+(b-t)
def pair_sum(p,q):
    s,e=two_sum(p[0],q[0])
    e=e+(p[1]+q[1])
    h=s+e
    return h,e-(h-s)
def pair_product(a,b):
    p=a*b
    ah,bh=rounded(a),rounded(b)
    al,bl=a-ah,b-bh
    return p,((ah*bh-p)+ah*bl+al*bh)+al*bl
def fold(parts):
    while len(parts)>1:
        parts=[pair_sum(*parts[i:i+2]) if i+1<len(parts) else parts[i] for i in range(0,len(parts),2)]
    return parts[0]
def down(p):
    m=p[0].shape[0]//8
    p=fold([(p[0][8*i:8*i+8],p[1][8*i:8*i+8]) for i in range(m)])
    for by in (4,2,1):
        p=pair_sum(p,(pltpu.roll(p[0],by,0),pltpu.roll(p[1],by,0)))
    return p[0][0:1],p[1][0:1]
def across(by_row):
    lane=lax.broadcasted_iota(jnp.int32,(32,SEG),1)//32
    out=by_row[0:32]
    for s in range(1,SYSTEMS):
        out=jnp.where(lane==s,by_row[32*s:32*s+32],out)
    return out
def gram(b):
    slices=[]
    rest=b
    for bits in (4,12,20,28):
        q=jnp.floor(rest*2.0**bits+0.5)*2.0**-bits
        rest=rest-q
        slices.append(q.astype(bf16))
    total=None
    for level in range(5):
        pairs=[(i,level-i) for i in range(4) if 0<=level-i<4]
        left=jnp.concatenate([slices[i] for i,_ in pairs],axis=1)
        right=jnp.concatenate([slices[j] for _,j in pairs],axis=1)
        part=across(contract(left,right,(1,1)))
        exact=(part,jnp.zeros_like(part))
        total=exact if total is None else pair_sum(total,exact)
    return total[0]*(1.0/PANELS),total[1]*(1.0/PANELS)
def payload(a,bt):
    lane=lax.broadcasted_iota(jnp.int32,(SEG,SEG),1)%32
    at=jnp.concatenate([jnp.broadcast_to(a[s:s+1],(32,SEG)) for s in range(SYSTEMS)],axis=0).T
    h,l=down(pair_product(at,jnp.where(lane==KRYLOV,at,bt)))
    return h*(1.0 / PANELS),l*(1.0 / PANELS)
def finish(a,p,g,bmat):
    k=lax.broadcasted_iota(jnp.int32,(1,SEG),1)%32
    system=lax.broadcasted_iota(jnp.int32,(8,SEG),0)
    lane=lax.broadcasted_iota(jnp.int32,(8,SEG),1)
    own=lane//32==system
    def times(c):
        column=across(jnp.broadcast_to(c,(SEG,SEG)).T)
        h,l=pair_product(g[0],column)
        return down((h,l+g[1]*column))
    basis_lane=k<KRYLOV
    fh,fl=jnp.where(basis_lane,p[0],0.0),jnp.where(basis_lane,p[1],0.0)
    gf=times(fh)
    second=(fh-gf[0])+(fl-gf[1])
    c=fh+second
    a8=jnp.concatenate([a,jnp.zeros((4,SEG),f32)],axis=0)
    twice=a8-contract(jnp.where(own,jnp.broadcast_to(c,(8,SEG)),0.0),bmat,(1,0),precision=HIGHEST)
    gc=times(c)
    u=pair_sum(gc,(-2.0*fh,-2.0*fl))
    h,l=pair_product(c,u[0])
    l=l+c*u[1]
    square=(jnp.where(k==KRYLOV,p[0],h),jnp.where(k==KRYLOV,p[1],l))
    for by in (1,2,4,8,16):
        square=pair_sum(square,(pltpu.roll(square[0],by,1),pltpu.roll(square[1],by,1)))
    length=jnp.sqrt(jnp.maximum(square[0]+square[1],0.0)+EPSILON)
    each=jnp.sum(jnp.where(own&(lane%32==31),jnp.broadcast_to(length,(8,SEG)),0.0),axis=1,keepdims=True)
    new=(twice/jnp.where(system[:,0:1]<SYSTEMS,each,1.0))[0:SYSTEMS]
    return new,jnp.where(k==KRYLOV,pltpu.roll(length,SEG-1,1),c)


def step_kernel(
    centroids, weight, basis, source_sel, target_sel, new_vector, hessenberg,
    src, tgt, feat, meet, vecs, sums, part, landed, bmat, bmat_t, gram_out, gram_in, gram_z, gram_all,
    dots_z, dots_q, send_sem, recv_sem,
):
    r, c = lax.axis_index("row"), lax.axis_index("col")
    z, q = c // 2, 2 * r + lax.rem(c, 2)

    def on_line(i):
        return r, lax.rem(c + 2 * i, 2 * DEPTH)

    def on_plane(to):
        return to // 2, 2 * z + lax.rem(to, 2)

    def near_offset(i):
        return lax.rem(DEPTH - REACH - 1 + i + lax.select(i > REACH, 1, 0), DEPTH)

    barrier = pltpu.get_barrier_semaphore()

    @pl.loop(1, 2 * REACH + 1)
    def _(i):
        pl.semaphore_signal(
            barrier, inc=1, device_id=on_line(near_offset(i)), device_id_type=MESH
        )

    @pl.loop(1, PLANE)
    def _(i):
        pl.semaphore_signal(
            barrier, inc=1, device_id=on_plane(lax.rem(q + i, PLANE)), device_id_type=MESH
        )

    def send(piece, place, sem, device):
        pltpu.make_async_remote_copy(
            src_ref=piece, dst_ref=place, send_sem=send_sem.at[sem], recv_sem=recv_sem.at[sem],
            device_id=device, device_id_type=MESH,
        ).start()

    def to_line(buf, sem):
        @pl.loop(1, DEPTH)
        def _(i):
            send(buf.at[z], buf.at[z], sem, on_line(i))

    def to_plane(buf, sem):
        @pl.loop(1, PLANE)
        def _(i):
            send(buf.at[q], buf.at[q], sem, on_plane(lax.rem(q + i, PLANE)))

    def settle(buf, count, sem):
        view = buf.at[pl.ds(0, count)]
        pltpu.make_async_copy(view, view, sem).wait()

    own_slot = 3
    src[own_slot, 0:3, :] = centroids[...]
    src[own_slot, 3:4, :] = weight[...]
    for s in range(SYSTEMS):
        src[own_slot, 4 + s : 5 + s, :] = basis[s, KRYLOV - 1 : KRYLOV, :]
    tgt[q, 0:3, :] = centroids[...]
    tgt[q, 3:4, :] = weight[...]
    load_basis(basis, bmat)
    bmat_t[...] = bmat[...].T
    gram_high, gram_low = gram(bmat[...])
    for k in range(PLANE):
        gram_out[k, 0:1, :] = gram_high[k : k + 1]
        gram_out[k, 1:2, :] = gram_low[k : k + 1]

    pl.semaphore_wait(barrier, 2 * REACH + PLANE - 1)

    def to_slot(i, sem):
        send(src.at[own_slot], src.at[lax.rem(i + own_slot, DEPTH)], sem, on_line(i))

    @pl.loop(2, 2 * REACH + 1)
    def _(i):
        to_slot(near_offset(i), 0)

    to_plane(tgt, 2)
    to_slot(DEPTH - REACH, 1)

    gram_in[q] = gram_out[q]

    @pl.loop(1, PLANE)
    def _(i):
        to = lax.rem(q + i, PLANE)
        send(gram_out.at[to], gram_in.at[q], 3, on_plane(to))

    def prepare(slots):
        for b in slots:
            block = src[b]
            pieces = pieces_of(block, block[3:4] * CORE)
            rows = slice(b * SEG, (b + 1) * SEG)
            feat[rows, :] = contract(pieces, source_sel[...], (0, 1)).astype(bf16)
            scaled = block[4:8] * (block[3:4] * (1.0 / PANELS**0.5))
            high = rounded(scaled)
            vecs[:, rows] = jnp.concatenate(
                [high, scaled - high, jnp.zeros((8, SEG), f32)], axis=0
            ).astype(bf16)

    def operate(meets, total, slots):
        for b in range(slots[0] // 2, slots[1] // 2):
            rows = slice(b * CHUNK, (b + 1) * CHUNK)
            entry = lax.rsqrt(contract(feat[rows, :], meets, (1, 0)))
            high = entry.astype(bf16)
            low = (entry - high.astype(f32)).astype(bf16)
            total = total + contract(vecs[:, rows], high, (1, 0))
            total = total + contract(vecs[:, rows], low, (1, 0))
        return total

    settle(src, NEAR - 1, recv_sem.at[0])
    ahead, behind = REACH, REACH - 1
    send(
        src.at[pl.ds(own_slot + 1, ahead)], src.at[pl.ds(own_slot + 1 + REACH, ahead)],
        1, on_line(REACH),
    )
    send(
        src.at[pl.ds(own_slot - behind, behind)],
        src.at[pl.ds(DEPTH - 1 - behind, behind)],
        1, on_line(DEPTH - REACH),
    )
    prepare(range(NEAR))
    settle(tgt, PLANE - 1, recv_sem.at[2])

    @pl.loop(0, ROWS // 4)
    def _(step):
        for i in range(4):
            pieces = []
            for core in range(2):
                block = tgt[2 * (4 * step + i) + core]
                block = jnp.concatenate([block, jnp.zeros((4, SEG), f32)], axis=0)
                pieces.append(pieces_of(block, 0.0))
            pieces = jnp.concatenate(pieces, axis=1)
            meet[4 * step + i] = contract(target_sel[...], pieces, (1, 0)).astype(bf16)

    @pl.loop(0, ROWS // 4)
    def _(step):
        for i in range(4):
            at = 4 * step + i
            sums[at] = operate(meet[at], jnp.zeros((16, CHUNK), f32), (0, NEAR))

    def collect(buf, count):
        return fold([(buf[i, 0:1, :], buf[i, 1:2, :]) for i in range(count)])

    settle(gram_in, PLANE - 1, recv_sem.at[3])
    high, low = collect(gram_in, PLANE)
    gram_z[z, 0:1, :] = high
    gram_z[z, 1:2, :] = low
    to_line(gram_z, 4)

    settle(src, DEPTH - NEAR, recv_sem.at[1])
    prepare(range(NEAR, DEPTH))

    def chosen(step, options):
        value = options[-1]
        for at in range(len(options) - 1):
            value = lax.select(step == at, options[at], value)
        return value

    def other_chip(step, i):
        x = lax.rem(r // 4 + chosen(step, [pair[0] for pair in OUTWARD[i]]), 4)
        y = lax.rem(lax.rem(r, 4) + chosen(step, [pair[1] for pair in OUTWARD[i]]), 4)
        return 4 * x + y

    @pl.loop(0, ROWS // 4)
    def _(step):
        for i in range(4):
            other = other_chip(step, i)
            total = operate(meet[other], sums[other], (NEAR, DEPTH))
            total = total[0:4] + total[4:8]
            part[2 * other] = total[:, 0:SEG]
            part[2 * other + 1] = total[:, SEG:CHUNK]
        for i in range(4):
            for core in range(2):
                to = 2 * other_chip(step, i) + core

                @pl.when(to != q)
                def _():
                    send(part.at[to], landed.at[q], 6, on_plane(to))

    landed[q] = part[q]
    settle(landed, PLANE - 1, recv_sem.at[6])
    applied = jnp.sum(landed[...], axis=0)

    high, low = payload(applied, bmat_t[...])
    dots_z[z, 0:1, :] = high
    dots_z[z, 1:2, :] = low
    to_line(dots_z, 7)
    settle(gram_z, DEPTH - 1, recv_sem.at[4])
    high, low = collect(gram_z, DEPTH)
    gram_all[q, 0:1, :] = high
    gram_all[q, 1:2, :] = low
    to_plane(gram_all, 5)
    settle(dots_z, DEPTH - 1, recv_sem.at[7])
    high, low = collect(dots_z, DEPTH)
    dots_q[q, 0:1, :] = high
    dots_q[q, 1:2, :] = low
    to_plane(dots_q, 8)
    settle(gram_all, PLANE - 1, recv_sem.at[5])
    gram_high = jnp.concatenate([gram_all[k, 0:1, :] for k in range(PLANE)], axis=0)
    gram_low = jnp.concatenate([gram_all[k, 1:2, :] for k in range(PLANE)], axis=0)
    settle(dots_q, PLANE - 1, recv_sem.at[8])
    vector, column = finish(applied, collect(dots_q, PLANE), (gram_high, gram_low), bmat[...])
    new_vector[...] = vector
    for s in range(SYSTEMS):
        hessenberg[s : s + 1, :] = column[:, 32 * s : 32 * s + KRYLOV + 1]

    settle(src, NEAR - 1, send_sem.at[0])
    settle(src, DEPTH - NEAR, send_sem.at[1])
    settle(tgt, PLANE - 1, send_sem.at[2])
    settle(gram_in, PLANE - 1, send_sem.at[3])
    settle(gram_z, DEPTH - 1, send_sem.at[4])
    settle(gram_all, PLANE - 1, send_sem.at[5])
    settle(landed, PLANE - 1, send_sem.at[6])
    settle(dots_z, DEPTH - 1, send_sem.at[7])
    settle(dots_q, PLANE - 1, send_sem.at[8])

def per_device(centroids, weight, basis):
    source, target = selections()
    vmem = pl.BlockSpec(memory_space=pltpu.VMEM)
    return pl.pallas_call(
        step_kernel,
        out_shape=(
            jax.ShapeDtypeStruct((SYSTEMS, SEG), f32),
            jax.ShapeDtypeStruct((SYSTEMS, KRYLOV + 1), f32),
        ),
        in_specs=[vmem] * 5,
        out_specs=(vmem, vmem),
        scratch_shapes=[
            pltpu.VMEM((DEPTH, 8, SEG), f32),
            pltpu.VMEM((PLANE, 4, SEG), f32),
            pltpu.VMEM((SOURCES, FEATURES), bf16),
            pltpu.VMEM((ROWS, FEATURES, CHUNK), bf16),
            pltpu.VMEM((16, SOURCES), bf16),
            pltpu.VMEM((ROWS, 16, CHUNK), f32),
            pltpu.VMEM((PLANE, 4, SEG), f32),
            pltpu.VMEM((PLANE, 4, SEG), f32),
            pltpu.VMEM((SEG, SEG), f32),
            pltpu.VMEM((SEG, SEG), f32),
            pltpu.VMEM((PLANE, 2, SEG), f32),
            pltpu.VMEM((PLANE, 2, SEG), f32),
            pltpu.VMEM((DEPTH, 2, SEG), f32),
            pltpu.VMEM((PLANE, 2, SEG), f32),
            pltpu.VMEM((DEPTH, 2, SEG), f32),
            pltpu.VMEM((PLANE, 2, SEG), f32),
            pltpu.SemaphoreType.DMA((9,)),
            pltpu.SemaphoreType.DMA((9,)),
        ],
        compiler_params=pltpu.CompilerParams(
            collective_id=0, has_side_effects=True, vmem_limit_bytes=40 * 2**20
        ),
        name="arnoldi_step",
    )(centroids, weight.reshape(1, SEG), basis, jnp.asarray(source, bf16), jnp.asarray(target, bf16))


def solution(mesh):
    placed = (P(None, ("col", "row")), P(("col", "row")), P(None, None, ("col", "row")))
    return jax.shard_map(
        per_device,
        mesh=mesh,
        in_specs=placed,
        out_specs=(P(None, ("col", "row")), P()),
        check_vma=False,
    )
```

```python
import functools

import jax
import jax.numpy as jnp
import numpy as np
from jax import lax
from jax.experimental import pallas as pl
from jax.experimental.pallas import tpu as pltpu
from jax.sharding import PartitionSpec as P

MESH = pl.DeviceIdType.MESH
f32, bf16 = jnp.float32, jnp.bfloat16
HIGHEST = lax.Precision.HIGHEST

SYSTEMS = 4
KRYLOV = 30
SEG = 128
ROWS = 16
COLS = 32
PANELS = SEG * ROWS * COLS
SOURCES = ROWS * SEG
CHUNK = 256
FEATURES = 128
CORE = 16.0 / PANELS
DEPTH = 16
PLANE = 32
NEAR = 8
REACH = 4
OUTWARD = (
    (2, 2), (2, 1), (2, 3), (1, 2), (3, 2), (1, 1), (1, 3), (3, 1),
    (3, 3), (2, 0), (0, 2), (1, 0), (3, 0), (0, 1), (0, 3), (0, 0),
)
EPSILON = 1e-06


def selections():
    source = np.zeros((FEATURES, 48), np.float32)
    target = np.zeros((FEATURES, 48), np.float32)
    coarse, fine, one = (0, 8), (16, 24), 38

    def products(at, lefts, rights):
        for left in lefts:
            for right in rights:
                for axis in range(3):
                    source[at, left + axis] = 1
                    target[at, right + axis] = -2
                    at += 1
        return at

    def norms(at, pieces):
        for piece in pieces:
            source[at, piece] = target[at, one] = 1
            source[at + 1, one] = target[at + 1, piece] = 1
            at += 2
        return at

    norms(products(0, coarse, coarse), (32, 33, 34))
    at = products(32, coarse, fine)
    at = products(at, fine, coarse + fine)
    norms(at, (35, 36, 37))
    return source, target


def rounded(a):
    return a.astype(bf16).astype(f32)


def pieces_of(points, extra):
    at = lax.broadcasted_iota(jnp.int32, (8, SEG), 0)
    points = jnp.where(at < 3, points, 0.0)
    coarse = jnp.floor(points * 128.0 + 0.5) * (1.0 / 128.0)
    fine = points - coarse
    coarse_high = rounded(coarse)
    fine_high = rounded(fine)
    fine_low = rounded(fine - fine_high)
    norm = jnp.sum(coarse * coarse, axis=0, keepdims=True)
    rest = jnp.sum(2.0 * coarse * fine + fine * fine, axis=0, keepdims=True) + extra
    tail = jnp.where(at == 6, 1.0, 0.0)
    row = 0
    for whole in (norm, rest):
        for _ in range(3):
            piece = rounded(whole)
            tail = jnp.where(at == row, piece, tail)
            whole = whole - piece
            row += 1
    rows = [coarse_high, coarse - coarse_high, fine_high, fine_low, tail, jnp.zeros((8, SEG), f32)]
    return jnp.concatenate(rows, axis=0).astype(bf16)


def contract(a, b, dims, **kw):
    return lax.dot_general(a, b, ((dims[:1], dims[1:]), ((), ())), preferred_element_type=f32, **kw)


def load_basis(basis,bmat):
    bmat[...]=jnp.zeros_like(bmat)
    for s in range(SYSTEMS):
        bmat[32*s:32*s+KRYLOV,:]=basis[s]
def two_sum(a,b):
    s=a+b
    t=s-a
    return s,(a-(s-t))+(b-t)
def pair_sum(p,q):
    s,e=two_sum(p[0],q[0])
    e=e+(p[1]+q[1])
    h=s+e
    return h,e-(h-s)
def pair_product(a,b):
    p=a*b
    ah,bh=rounded(a),rounded(b)
    al,bl=a-ah,b-bh
    return p,((ah*bh-p)+ah*bl+al*bh)+al*bl
def fold(parts):
    while len(parts)>1:
        parts=[pair_sum(*parts[i:i+2]) if i+1<len(parts) else parts[i] for i in range(0,len(parts),2)]
    return parts[0]
def down(p):
    m=p[0].shape[0]//8
    p=fold([(p[0][8*i:8*i+8],p[1][8*i:8*i+8]) for i in range(m)])
    for by in (4,2,1):
        p=pair_sum(p,(pltpu.roll(p[0],by,0),pltpu.roll(p[1],by,0)))
    return p[0][0:1],p[1][0:1]
def across(by_row):
    lane=lax.broadcasted_iota(jnp.int32,(32,SEG),1)//32
    out=by_row[0:32]
    for s in range(1,SYSTEMS):
        out=jnp.where(lane==s,by_row[32*s:32*s+32],out)
    return out
def gram(b):
    slices=[]
    rest=b
    for bits in (4,12,20,28):
        q=jnp.floor(rest*2.0**bits+0.5)*2.0**-bits
        rest=rest-q
        slices.append(q.astype(bf16))
    total=None
    for level in range(5):
        pairs=[(i,level-i) for i in range(4) if 0<=level-i<4]
        left=jnp.concatenate([slices[i] for i,_ in pairs],axis=1)
        right=jnp.concatenate([slices[j] for _,j in pairs],axis=1)
        part=across(contract(left,right,(1,1)))
        exact=(part,jnp.zeros_like(part))
        total=exact if total is None else pair_sum(total,exact)
    return total[0]*(1.0/PANELS),total[1]*(1.0/PANELS)
def payload(a,bt):
    lane=lax.broadcasted_iota(jnp.int32,(SEG,SEG),1)%32
    at=jnp.concatenate([jnp.broadcast_to(a[s:s+1],(32,SEG)) for s in range(SYSTEMS)],axis=0).T
    h,l=down(pair_product(at,jnp.where(lane==KRYLOV,at,bt)))
    return h*(1.0 / PANELS),l*(1.0 / PANELS)
def finish(a,p,g,bmat):
    k=lax.broadcasted_iota(jnp.int32,(1,SEG),1)%32
    system=lax.broadcasted_iota(jnp.int32,(8,SEG),0)
    lane=lax.broadcasted_iota(jnp.int32,(8,SEG),1)
    own=lane//32==system
    def times(c):
        column=across(jnp.broadcast_to(c,(SEG,SEG)).T)
        h,l=pair_product(g[0],column)
        return down((h,l+g[1]*column))
    basis_lane=k<KRYLOV
    fh,fl=jnp.where(basis_lane,p[0],0.0),jnp.where(basis_lane,p[1],0.0)
    gf=times(fh)
    second=(fh-gf[0])+(fl-gf[1])
    c=fh+second
    a8=jnp.concatenate([a,jnp.zeros((4,SEG),f32)],axis=0)
    twice=a8-contract(jnp.where(own,jnp.broadcast_to(c,(8,SEG)),0.0),bmat,(1,0),precision=HIGHEST)
    gc=times(c)
    u=pair_sum(gc,(-2.0*fh,-2.0*fl))
    h,l=pair_product(c,u[0])
    l=l+c*u[1]
    square=(jnp.where(k==KRYLOV,p[0],h),jnp.where(k==KRYLOV,p[1],l))
    for by in (1,2,4,8,16):
        square=pair_sum(square,(pltpu.roll(square[0],by,1),pltpu.roll(square[1],by,1)))
    length=jnp.sqrt(jnp.maximum(square[0]+square[1],0.0)+EPSILON)
    each=jnp.sum(jnp.where(own&(lane%32==31),jnp.broadcast_to(length,(8,SEG)),0.0),axis=1,keepdims=True)
    new=(twice/jnp.where(system[:,0:1]<SYSTEMS,each,1.0))[0:SYSTEMS]
    return new,jnp.where(k==KRYLOV,pltpu.roll(length,SEG-1,1),c)


def step_kernel(
    centroids, weight, basis, source_sel, target_sel, new_vector, hessenberg,
    src, tgt, feat, meet, vecs, sums, part, landed, bmat, bmat_t, gram_out, gram_in, gram_z, gram_all,
    dots_z, dots_q, send_sem, recv_sem,
):
    r, c = lax.axis_index("row"), lax.axis_index("col")
    z, q = c // 2, 2 * r + lax.rem(c, 2)

    def on_line(i):
        return r, lax.rem(c + 2 * i, 2 * DEPTH)

    def on_plane(to):
        return to // 2, 2 * z + lax.rem(to, 2)

    def near_offset(i):
        return lax.rem(DEPTH - REACH - 1 + i + lax.select(i > REACH, 1, 0), DEPTH)

    barrier = pltpu.get_barrier_semaphore()

    @pl.loop(1, 2 * REACH + 1)
    def _(i):
        pl.semaphore_signal(
            barrier, inc=1, device_id=on_line(near_offset(i)), device_id_type=MESH
        )

    @pl.loop(1, PLANE)
    def _(i):
        pl.semaphore_signal(
            barrier, inc=1, device_id=on_plane(lax.rem(q + i, PLANE)), device_id_type=MESH
        )

    def send(piece, place, sem, device):
        pltpu.make_async_remote_copy(
            src_ref=piece, dst_ref=place, send_sem=send_sem.at[sem], recv_sem=recv_sem.at[sem],
            device_id=device, device_id_type=MESH,
        ).start()

    def to_line(buf, sem):
        @pl.loop(1, DEPTH)
        def _(i):
            send(buf.at[z], buf.at[z], sem, on_line(i))

    def to_plane(buf, sem):
        @pl.loop(1, PLANE)
        def _(i):
            send(buf.at[q], buf.at[q], sem, on_plane(lax.rem(q + i, PLANE)))

    def settle(buf, count, sem):
        view = buf.at[pl.ds(0, count)]
        pltpu.make_async_copy(view, view, sem).wait()

    own_slot = 3
    src[own_slot, 0:3, :] = centroids[...]
    src[own_slot, 3:4, :] = weight[...]
    for s in range(SYSTEMS):
        src[own_slot, 4 + s : 5 + s, :] = basis[s, KRYLOV - 1 : KRYLOV, :]
    tgt[q, 0:3, :] = centroids[...]
    tgt[q, 3:4, :] = weight[...]

    pl.semaphore_wait(barrier, 2 * REACH + PLANE - 1)

    def to_slot(i, sem):
        send(src.at[own_slot], src.at[lax.rem(i + own_slot, DEPTH)], sem, on_line(i))

    @pl.loop(2, 2 * REACH + 1)
    def _(i):
        to_slot(near_offset(i), 0)

    to_plane(tgt, 2)
    to_slot(DEPTH - REACH, 1)

    load_basis(basis, bmat)
    bmat_t[...] = bmat[...].T
    gram_high, gram_low = gram(bmat[...])
    for k in range(PLANE):
        gram_out[k, 0:1, :] = gram_high[k : k + 1]
        gram_out[k, 1:2, :] = gram_low[k : k + 1]
    gram_in[q] = gram_out[q]

    @pl.loop(1, PLANE)
    def _(i):
        to = lax.rem(q + i, PLANE)
        send(gram_out.at[to], gram_in.at[q], 3, on_plane(to))

    def prepare(slots):
        for b in slots:
            block = src[b]
            pieces = pieces_of(block, block[3:4] * CORE)
            rows = slice(b * SEG, (b + 1) * SEG)
            feat[rows, :] = contract(pieces, source_sel[...], (0, 1)).astype(bf16)
            scaled = block[4:8] * (block[3:4] * (1.0 / PANELS**0.5))
            high = rounded(scaled)
            vecs[:, rows] = jnp.concatenate(
                [high, scaled - high, jnp.zeros((8, SEG), f32)], axis=0
            ).astype(bf16)

    def operate(meets, total, slots):
        for b in range(slots[0] // 2, slots[1] // 2):
            rows = slice(b * CHUNK, (b + 1) * CHUNK)
            entry = lax.rsqrt(contract(feat[rows, :], meets, (1, 0)))
            high = entry.astype(bf16)
            low = (entry - high.astype(f32)).astype(bf16)
            total = total + contract(vecs[:, rows], high, (1, 0))
            total = total + contract(vecs[:, rows], low, (1, 0))
        return total

    settle(src, NEAR - 1, recv_sem.at[0])
    ahead, behind = REACH, REACH - 1
    send(
        src.at[pl.ds(own_slot + 1, ahead)], src.at[pl.ds(own_slot + 1 + REACH, ahead)],
        1, on_line(REACH),
    )
    send(
        src.at[pl.ds(own_slot - behind, behind)],
        src.at[pl.ds(DEPTH - 1 - behind, behind)],
        1, on_line(DEPTH - REACH),
    )
    prepare(range(NEAR))
    settle(tgt, PLANE - 1, recv_sem.at[2])

    def other_chip(shift):
        return 4 * lax.rem(r // 4 + shift[0], 4) + lax.rem(lax.rem(r, 4) + shift[1], 4)

    def chosen(step, options):
        value = options[-1]
        for at in range(len(options) - 1):
            value = lax.select(step == at, options[at], value)
        return value

    @pl.loop(0, ROWS // 4)
    def _(step):
        for i in range(4):
            shift = [chosen(step, [pair[axis] for pair in OUTWARD[i::4]]) for axis in range(2)]
            other = other_chip(shift)
            pieces = []
            for core in range(2):
                block = jnp.concatenate([tgt[2 * other + core], jnp.zeros((4, SEG), f32)], axis=0)
                pieces.append(pieces_of(block, 0.0))
            pieces = jnp.concatenate(pieces, axis=1)
            meet[4 * step + i] = contract(target_sel[...], pieces, (1, 0)).astype(bf16)

    nothing = jnp.zeros((16, CHUNK), f32)

    @pl.loop(0, (ROWS - 1) // 5)
    def _(step):
        for i in range(5):
            at = 5 * step + i
            sums[at] = operate(meet[at], nothing, (0, NEAR))

    def collect(buf, count):
        return fold([(buf[i, 0:1, :], buf[i, 1:2, :]) for i in range(count)])

    settle(src, DEPTH - NEAR, recv_sem.at[1])
    prepare(range(NEAR, DEPTH))

    def finished(at, other):
        total = operate(meet[at], sums[at], (NEAR, DEPTH))
        total = total[0:4] + total[4:8]
        part[2 * other] = total[:, 0:SEG]
        part[2 * other + 1] = total[:, SEG:CHUNK]

    def deliver(to):
        send(part.at[to], landed.at[q], 6, on_plane(to))

    @pl.loop(0, (ROWS - 1) // 5)
    def _(step):
        others = []
        for i in range(5):
            shifts = OUTWARD[i : ROWS - 1 : 5]
            others.append(other_chip([chosen(step, [p[axis] for p in shifts]) for axis in range(2)]))
            finished(5 * step + i, others[-1])
        for other in others:
            deliver(2 * other)
            deliver(2 * other + 1)

    sums[ROWS - 1] = operate(meet[ROWS - 1], nothing, (0, NEAR))
    finished(ROWS - 1, r)
    deliver(2 * r + 1 - lax.rem(c, 2))
    landed[q] = part[q]
    settle(gram_in, PLANE - 1, recv_sem.at[3])
    high, low = collect(gram_in, PLANE)
    gram_z[z, 0:1, :] = high
    gram_z[z, 1:2, :] = low
    to_line(gram_z, 4)

    settle(landed, PLANE - 1, recv_sem.at[6])
    applied = jnp.sum(landed[...], axis=0)

    high, low = payload(applied, bmat_t[...])
    dots_z[z, 0:1, :] = high
    dots_z[z, 1:2, :] = low
    to_line(dots_z, 7)
    settle(gram_z, DEPTH - 1, recv_sem.at[4])
    high, low = collect(gram_z, DEPTH)
    gram_all[q, 0:1, :] = high
    gram_all[q, 1:2, :] = low
    to_plane(gram_all, 5)
    settle(dots_z, DEPTH - 1, recv_sem.at[7])
    high, low = collect(dots_z, DEPTH)
    dots_q[q, 0:1, :] = high
    dots_q[q, 1:2, :] = low
    to_plane(dots_q, 8)
    settle(gram_all, PLANE - 1, recv_sem.at[5])
    gram_high = jnp.concatenate([gram_all[k, 0:1, :] for k in range(PLANE)], axis=0)
    gram_low = jnp.concatenate([gram_all[k, 1:2, :] for k in range(PLANE)], axis=0)
    settle(dots_q, PLANE - 1, recv_sem.at[8])
    vector, column = finish(applied, collect(dots_q, PLANE), (gram_high, gram_low), bmat[...])
    new_vector[...] = vector
    for s in range(SYSTEMS):
        hessenberg[s : s + 1, :] = column[:, 32 * s : 32 * s + KRYLOV + 1]

    settle(src, NEAR - 1, send_sem.at[0])
    settle(src, DEPTH - NEAR, send_sem.at[1])
    settle(tgt, PLANE - 1, send_sem.at[2])
    settle(gram_in, PLANE - 1, send_sem.at[3])
    settle(gram_z, DEPTH - 1, send_sem.at[4])
    settle(gram_all, PLANE - 1, send_sem.at[5])
    settle(landed, PLANE - 1, send_sem.at[6])
    settle(dots_z, DEPTH - 1, send_sem.at[7])
    settle(dots_q, PLANE - 1, send_sem.at[8])

def per_device(centroids, weight, basis):
    source, target = selections()
    vmem = pl.BlockSpec(memory_space=pltpu.VMEM)
    return pl.pallas_call(
        step_kernel,
        out_shape=(
            jax.ShapeDtypeStruct((SYSTEMS, SEG), f32),
            jax.ShapeDtypeStruct((SYSTEMS, KRYLOV + 1), f32),
        ),
        in_specs=[vmem] * 5,
        out_specs=(vmem, vmem),
        scratch_shapes=[
            pltpu.VMEM((DEPTH, 8, SEG), f32),
            pltpu.VMEM((PLANE, 4, SEG), f32),
            pltpu.VMEM((SOURCES, FEATURES), bf16),
            pltpu.VMEM((ROWS, FEATURES, CHUNK), bf16),
            pltpu.VMEM((16, SOURCES), bf16),
            pltpu.VMEM((ROWS, 16, CHUNK), f32),
            pltpu.VMEM((PLANE, 4, SEG), f32),
            pltpu.VMEM((PLANE, 4, SEG), f32),
            pltpu.VMEM((SEG, SEG), f32),
            pltpu.VMEM((SEG, SEG), f32),
            pltpu.VMEM((PLANE, 2, SEG), f32),
            pltpu.VMEM((PLANE, 2, SEG), f32),
            pltpu.VMEM((DEPTH, 2, SEG), f32),
            pltpu.VMEM((PLANE, 2, SEG), f32),
            pltpu.VMEM((DEPTH, 2, SEG), f32),
            pltpu.VMEM((PLANE, 2, SEG), f32),
            pltpu.SemaphoreType.DMA((9,)),
            pltpu.SemaphoreType.DMA((9,)),
        ],
        compiler_params=pltpu.CompilerParams(
            collective_id=0, has_side_effects=True, vmem_limit_bytes=40 * 2**20
        ),
        name="arnoldi_step",
    )(centroids, weight.reshape(1, SEG), basis, jnp.asarray(source, bf16), jnp.asarray(target, bf16))


def solution(mesh):
    placed = (P(None, ("col", "row")), P(("col", "row")), P(None, None, ("col", "row")))
    return jax.shard_map(
        per_device,
        mesh=mesh,
        in_specs=placed,
        out_specs=(P(None, ("col", "row")), P()),
        check_vma=False,
    )
```

```python
import functools

import jax
import jax.numpy as jnp
import numpy as np
from jax import lax
from jax.experimental import pallas as pl
from jax.experimental.pallas import tpu as pltpu
from jax.sharding import PartitionSpec as P

MESH = pl.DeviceIdType.MESH
f32, bf16 = jnp.float32, jnp.bfloat16
HIGHEST = lax.Precision.HIGHEST

SYSTEMS = 4
KRYLOV = 30
SEG = 128
ROWS = 16
COLS = 32
PANELS = SEG * ROWS * COLS
SOURCES = ROWS * SEG
CHUNK = 256
FEATURES = 128
CORE = 16.0 / PANELS
DEPTH = 16
PLANE = 32
NEAR = 8
REACH = 4
OUTWARD = (
    (2, 2), (2, 1), (2, 3), (1, 2), (3, 2), (1, 1), (1, 3), (3, 1),
    (3, 3), (2, 0), (0, 2), (1, 0), (3, 0), (0, 1), (0, 3), (0, 0),
)
EPSILON = 1e-06


def selections():
    source = np.zeros((FEATURES, 48), np.float32)
    target = np.zeros((FEATURES, 48), np.float32)
    coarse, fine, one = (0, 8), (16, 24), 38

    def products(at, lefts, rights):
        for left in lefts:
            for right in rights:
                for axis in range(3):
                    source[at, left + axis] = 1
                    target[at, right + axis] = -2
                    at += 1
        return at

    def norms(at, pieces):
        for piece in pieces:
            source[at, piece] = target[at, one] = 1
            source[at + 1, one] = target[at + 1, piece] = 1
            at += 2
        return at

    norms(products(0, coarse, coarse), (32, 33, 34))
    at = products(32, coarse, fine)
    at = products(at, fine, coarse + fine)
    norms(at, (35, 36, 37))
    return source, target


def rounded(a):
    return a.astype(bf16).astype(f32)


def pieces_of(points, extra):
    at = lax.broadcasted_iota(jnp.int32, (8, SEG), 0)
    points = jnp.where(at < 3, points, 0.0)
    coarse = jnp.floor(points * 128.0 + 0.5) * (1.0 / 128.0)
    fine = points - coarse
    coarse_high = rounded(coarse)
    fine_high = rounded(fine)
    fine_low = rounded(fine - fine_high)
    norm = jnp.sum(coarse * coarse, axis=0, keepdims=True)
    rest = jnp.sum(2.0 * coarse * fine + fine * fine, axis=0, keepdims=True) + extra
    tail = jnp.where(at == 6, 1.0, 0.0)
    row = 0
    for whole in (norm, rest):
        for _ in range(3):
            piece = rounded(whole)
            tail = jnp.where(at == row, piece, tail)
            whole = whole - piece
            row += 1
    rows = [coarse_high, coarse - coarse_high, fine_high, fine_low, tail, jnp.zeros((8, SEG), f32)]
    return jnp.concatenate(rows, axis=0).astype(bf16)


def contract(a, b, dims, **kw):
    return lax.dot_general(a, b, ((dims[:1], dims[1:]), ((), ())), preferred_element_type=f32, **kw)


def load_basis(basis,bmat):
    bmat[...]=jnp.zeros_like(bmat)
    for s in range(SYSTEMS):
        bmat[32*s:32*s+KRYLOV,:]=basis[s]
def two_sum(a,b):
    s=a+b
    t=s-a
    return s,(a-(s-t))+(b-t)
def pair_sum(p,q):
    s,e=two_sum(p[0],q[0])
    e=e+(p[1]+q[1])
    h=s+e
    return h,e-(h-s)
def pair_product(a,b):
    p=a*b
    ah,bh=rounded(a),rounded(b)
    al,bl=a-ah,b-bh
    return p,((ah*bh-p)+ah*bl+al*bh)+al*bl
def fold(parts):
    while len(parts)>1:
        parts=[pair_sum(*parts[i:i+2]) if i+1<len(parts) else parts[i] for i in range(0,len(parts),2)]
    return parts[0]
def down(p):
    m=p[0].shape[0]//8
    p=fold([(p[0][8*i:8*i+8],p[1][8*i:8*i+8]) for i in range(m)])
    for by in (4,2,1):
        p=pair_sum(p,(pltpu.roll(p[0],by,0),pltpu.roll(p[1],by,0)))
    return p[0][0:1],p[1][0:1]
def across(by_row):
    lane=lax.broadcasted_iota(jnp.int32,(32,SEG),1)//32
    out=by_row[0:32]
    for s in range(1,SYSTEMS):
        out=jnp.where(lane==s,by_row[32*s:32*s+32],out)
    return out
def gram(b):
    slices=[]
    rest=b
    for bits in (4,12,20,28):
        q=jnp.floor(rest*2.0**bits+0.5)*2.0**-bits
        rest=rest-q
        slices.append(q.astype(bf16))
    total=None
    for level in range(5):
        pairs=[(i,level-i) for i in range(4) if 0<=level-i<4]
        left=jnp.concatenate([slices[i] for i,_ in pairs],axis=1)
        right=jnp.concatenate([slices[j] for _,j in pairs],axis=1)
        part=across(contract(left,right,(1,1)))
        exact=(part,jnp.zeros_like(part))
        total=exact if total is None else pair_sum(total,exact)
    return total[0]*(1.0/PANELS),total[1]*(1.0/PANELS)
def payload(a,bt):
    lane=lax.broadcasted_iota(jnp.int32,(SEG,SEG),1)%32
    at=jnp.concatenate([jnp.broadcast_to(a[s:s+1],(32,SEG)) for s in range(SYSTEMS)],axis=0).T
    h,l=down(pair_product(at,jnp.where(lane==KRYLOV,at,bt)))
    return h*(1.0 / PANELS),l*(1.0 / PANELS)
def finish(a,p,g,bmat):
    k=lax.broadcasted_iota(jnp.int32,(1,SEG),1)%32
    system=lax.broadcasted_iota(jnp.int32,(8,SEG),0)
    lane=lax.broadcasted_iota(jnp.int32,(8,SEG),1)
    own=lane//32==system
    def times(c):
        column=across(jnp.broadcast_to(c,(SEG,SEG)).T)
        h,l=pair_product(g[0],column)
        return down((h,l+g[1]*column))
    basis_lane=k<KRYLOV
    fh,fl=jnp.where(basis_lane,p[0],0.0),jnp.where(basis_lane,p[1],0.0)
    gf=times(fh)
    second=(fh-gf[0])+(fl-gf[1])
    c=fh+second
    a8=jnp.concatenate([a,jnp.zeros((4,SEG),f32)],axis=0)
    twice=a8-contract(jnp.where(own,jnp.broadcast_to(c,(8,SEG)),0.0),bmat,(1,0),precision=HIGHEST)
    gc=times(c)
    u=pair_sum(gc,(-2.0*fh,-2.0*fl))
    h,l=pair_product(c,u[0])
    l=l+c*u[1]
    square=(jnp.where(k==KRYLOV,p[0],h),jnp.where(k==KRYLOV,p[1],l))
    for by in (1,2,4,8,16):
        square=pair_sum(square,(pltpu.roll(square[0],by,1),pltpu.roll(square[1],by,1)))
    length=jnp.sqrt(jnp.maximum(square[0]+square[1],0.0)+EPSILON)
    each=jnp.sum(jnp.where(own&(lane%32==31),jnp.broadcast_to(length,(8,SEG)),0.0),axis=1,keepdims=True)
    new=(twice/jnp.where(system[:,0:1]<SYSTEMS,each,1.0))[0:SYSTEMS]
    return new,jnp.where(k==KRYLOV,pltpu.roll(length,SEG-1,1),c)


def step_kernel(
    centroids, weight, basis, source_sel, target_sel, new_vector, hessenberg,
    src, tgt, feat, meet, vecs, sums, part, landed, bmat, bmat_t, gram_out, gram_in, gram_z, gram_all,
    dots_z, dots_q, send_sem, recv_sem,
):
    r, c = lax.axis_index("row"), lax.axis_index("col")
    z, q = c // 2, 2 * r + lax.rem(c, 2)

    def on_line(i):
        return r, lax.rem(c + 2 * i, 2 * DEPTH)

    def on_plane(to):
        return to // 2, 2 * z + lax.rem(to, 2)

    def near_offset(i):
        return lax.rem(DEPTH - REACH - 1 + i + lax.select(i > REACH, 1, 0), DEPTH)

    barrier = pltpu.get_barrier_semaphore()

    @pl.loop(1, 2 * REACH + 1)
    def _(i):
        pl.semaphore_signal(
            barrier, inc=1, device_id=on_line(near_offset(i)), device_id_type=MESH
        )

    @pl.loop(1, PLANE)
    def _(i):
        pl.semaphore_signal(
            barrier, inc=1, device_id=on_plane(lax.rem(q + i, PLANE)), device_id_type=MESH
        )

    def send(piece, place, sem, device):
        pltpu.make_async_remote_copy(
            src_ref=piece, dst_ref=place, send_sem=send_sem.at[sem], recv_sem=recv_sem.at[sem],
            device_id=device, device_id_type=MESH,
        ).start()

    def to_line(buf, sem):
        @pl.loop(1, DEPTH)
        def _(i):
            send(buf.at[z], buf.at[z], sem, on_line(i))

    def to_plane(buf, sem):
        @pl.loop(1, PLANE)
        def _(i):
            send(buf.at[q], buf.at[q], sem, on_plane(lax.rem(q + i, PLANE)))

    def settle(buf, count, sem):
        view = buf.at[pl.ds(0, count)]
        pltpu.make_async_copy(view, view, sem).wait()

    own_slot = 3
    src[own_slot, 0:3, :] = centroids[...]
    src[own_slot, 3:4, :] = weight[...]
    for s in range(SYSTEMS):
        src[own_slot, 4 + s : 5 + s, :] = basis[s, KRYLOV - 1 : KRYLOV, :]
    tgt[q, 0:3, :] = centroids[...]
    tgt[q, 3:4, :] = weight[...]

    pl.semaphore_wait(barrier, 2 * REACH + PLANE - 1)

    def to_slot(i, sem):
        send(src.at[own_slot], src.at[lax.rem(i + own_slot, DEPTH)], sem, on_line(i))

    @pl.loop(2, 2 * REACH + 1)
    def _(i):
        to_slot(near_offset(i), 0)

    to_plane(tgt, 2)
    to_slot(DEPTH - REACH, 1)

    load_basis(basis, bmat)
    bmat_t[...] = bmat[...].T
    gram_high, gram_low = gram(bmat[...])
    for k in range(PLANE):
        gram_out[k, 0:1, :] = gram_high[k : k + 1]
        gram_out[k, 1:2, :] = gram_low[k : k + 1]
    gram_in[q] = gram_out[q]

    @pl.loop(1, PLANE)
    def _(i):
        to = lax.rem(q + i, PLANE)
        send(gram_out.at[to], gram_in.at[q], 3, on_plane(to))

    def prepare(slots):
        for b in slots:
            block = src[b]
            pieces = pieces_of(block, block[3:4] * CORE)
            rows = slice(b * SEG, (b + 1) * SEG)
            feat[rows, :] = contract(pieces, source_sel[...], (0, 1)).astype(bf16)
            scaled = block[4:8] * (block[3:4] * (1.0 / PANELS**0.5))
            high = rounded(scaled)
            vecs[:, rows] = jnp.concatenate(
                [high, scaled - high, jnp.zeros((8, SEG), f32)], axis=0
            ).astype(bf16)

    def operate(meets, total, slots):
        for b in range(slots[0] // 2, slots[1] // 2):
            rows = slice(b * CHUNK, (b + 1) * CHUNK)
            entry = lax.rsqrt(contract(feat[rows, :], meets, (1, 0)))
            high = entry.astype(bf16)
            low = (entry - high.astype(f32)).astype(bf16)
            total = total + contract(vecs[:, rows], high, (1, 0))
            total = total + contract(vecs[:, rows], low, (1, 0))
        return total

    settle(src, NEAR - 1, recv_sem.at[0])
    ahead, behind = REACH, REACH - 1
    send(
        src.at[pl.ds(own_slot + 1, ahead)], src.at[pl.ds(own_slot + 1 + REACH, ahead)],
        1, on_line(REACH),
    )
    send(
        src.at[pl.ds(own_slot - behind, behind)],
        src.at[pl.ds(DEPTH - 1 - behind, behind)],
        1, on_line(DEPTH - REACH),
    )
    prepare(range(NEAR))
    settle(tgt, PLANE - 1, recv_sem.at[2])

    def other_chip(shift):
        return 4 * lax.rem(r // 4 + shift[0], 4) + lax.rem(lax.rem(r, 4) + shift[1], 4)

    def chosen(step, options):
        value = options[-1]
        for at in range(len(options) - 1):
            value = lax.select(step == at, options[at], value)
        return value

    for at in range(ROWS):
        other = other_chip(OUTWARD[at])
        pieces = []
        for core in range(2):
            block = jnp.concatenate([tgt[2 * other + core], jnp.zeros((4, SEG), f32)], axis=0)
            pieces.append(pieces_of(block, 0.0))
        pieces = jnp.concatenate(pieces, axis=1)
        meet[at] = contract(target_sel[...], pieces, (1, 0)).astype(bf16)

    nothing = jnp.zeros((16, CHUNK), f32)

    for at in range(ROWS - 1):
        sums[at] = operate(meet[at], nothing, (0, NEAR))

    def collect(buf, count):
        return fold([(buf[i, 0:1, :], buf[i, 1:2, :]) for i in range(count)])

    settle(src, DEPTH - NEAR, recv_sem.at[1])
    prepare(range(NEAR, DEPTH))

    def finished(at, other):
        total = operate(meet[at], sums[at], (NEAR, DEPTH))
        total = total[0:4] + total[4:8]
        part[2 * other] = total[:, 0:SEG]
        part[2 * other + 1] = total[:, SEG:CHUNK]

    def deliver(to):
        send(part.at[to], landed.at[q], 6, on_plane(to))

    @pl.loop(0, (ROWS - 1) // 5)
    def _(step):
        others = []
        for i in range(5):
            shifts = OUTWARD[i : ROWS - 1 : 5]
            others.append(other_chip([chosen(step, [p[axis] for p in shifts]) for axis in range(2)]))
            finished(5 * step + i, others[-1])
        for other in others:
            deliver(2 * other)
            deliver(2 * other + 1)

    sums[ROWS - 1] = operate(meet[ROWS - 1], nothing, (0, NEAR))
    finished(ROWS - 1, r)
    deliver(2 * r + 1 - lax.rem(c, 2))
    landed[q] = part[q]
    settle(gram_in, PLANE - 1, recv_sem.at[3])
    high, low = collect(gram_in, PLANE)
    gram_z[z, 0:1, :] = high
    gram_z[z, 1:2, :] = low
    to_line(gram_z, 4)

    settle(landed, PLANE - 1, recv_sem.at[6])
    applied = jnp.sum(landed[...], axis=0)

    high, low = payload(applied, bmat_t[...])
    dots_z[z, 0:1, :] = high
    dots_z[z, 1:2, :] = low
    to_line(dots_z, 7)
    settle(gram_z, DEPTH - 1, recv_sem.at[4])
    high, low = collect(gram_z, DEPTH)
    gram_all[q, 0:1, :] = high
    gram_all[q, 1:2, :] = low
    to_plane(gram_all, 5)
    settle(dots_z, DEPTH - 1, recv_sem.at[7])
    high, low = collect(dots_z, DEPTH)
    dots_q[q, 0:1, :] = high
    dots_q[q, 1:2, :] = low
    to_plane(dots_q, 8)
    settle(gram_all, PLANE - 1, recv_sem.at[5])
    gram_high = jnp.concatenate([gram_all[k, 0:1, :] for k in range(PLANE)], axis=0)
    gram_low = jnp.concatenate([gram_all[k, 1:2, :] for k in range(PLANE)], axis=0)
    settle(dots_q, PLANE - 1, recv_sem.at[8])
    vector, column = finish(applied, collect(dots_q, PLANE), (gram_high, gram_low), bmat[...])
    new_vector[...] = vector
    for s in range(SYSTEMS):
        hessenberg[s : s + 1, :] = column[:, 32 * s : 32 * s + KRYLOV + 1]

    settle(src, NEAR - 1, send_sem.at[0])
    settle(src, DEPTH - NEAR, send_sem.at[1])
    settle(tgt, PLANE - 1, send_sem.at[2])
    settle(gram_in, PLANE - 1, send_sem.at[3])
    settle(gram_z, DEPTH - 1, send_sem.at[4])
    settle(gram_all, PLANE - 1, send_sem.at[5])
    settle(landed, PLANE - 1, send_sem.at[6])
    settle(dots_z, DEPTH - 1, send_sem.at[7])
    settle(dots_q, PLANE - 1, send_sem.at[8])

def per_device(centroids, weight, basis):
    source, target = selections()
    vmem = pl.BlockSpec(memory_space=pltpu.VMEM)
    return pl.pallas_call(
        step_kernel,
        out_shape=(
            jax.ShapeDtypeStruct((SYSTEMS, SEG), f32),
            jax.ShapeDtypeStruct((SYSTEMS, KRYLOV + 1), f32),
        ),
        in_specs=[vmem] * 5,
        out_specs=(vmem, vmem),
        scratch_shapes=[
            pltpu.VMEM((DEPTH, 8, SEG), f32),
            pltpu.VMEM((PLANE, 4, SEG), f32),
            pltpu.VMEM((SOURCES, FEATURES), bf16),
            pltpu.VMEM((ROWS, FEATURES, CHUNK), bf16),
            pltpu.VMEM((16, SOURCES), bf16),
            pltpu.VMEM((ROWS, 16, CHUNK), f32),
            pltpu.VMEM((PLANE, 4, SEG), f32),
            pltpu.VMEM((PLANE, 4, SEG), f32),
            pltpu.VMEM((SEG, SEG), f32),
            pltpu.VMEM((SEG, SEG), f32),
            pltpu.VMEM((PLANE, 2, SEG), f32),
            pltpu.VMEM((PLANE, 2, SEG), f32),
            pltpu.VMEM((DEPTH, 2, SEG), f32),
            pltpu.VMEM((PLANE, 2, SEG), f32),
            pltpu.VMEM((DEPTH, 2, SEG), f32),
            pltpu.VMEM((PLANE, 2, SEG), f32),
            pltpu.SemaphoreType.DMA((9,)),
            pltpu.SemaphoreType.DMA((9,)),
        ],
        compiler_params=pltpu.CompilerParams(
            collective_id=0, has_side_effects=True, vmem_limit_bytes=40 * 2**20
        ),
        name="arnoldi_step",
    )(centroids, weight.reshape(1, SEG), basis, jnp.asarray(source, bf16), jnp.asarray(target, bf16))


def solution(mesh):
    placed = (P(None, ("col", "row")), P(("col", "row")), P(None, None, ("col", "row")))
    return jax.shard_map(
        per_device,
        mesh=mesh,
        in_specs=placed,
        out_specs=(P(None, ("col", "row")), P()),
        check_vma=False,
    )
```

```python
import functools

import jax
import jax.numpy as jnp
import numpy as np
from jax import lax
from jax.experimental import pallas as pl
from jax.experimental.pallas import tpu as pltpu
from jax.sharding import PartitionSpec as P

MESH = pl.DeviceIdType.MESH
f32, bf16 = jnp.float32, jnp.bfloat16
HIGHEST = lax.Precision.HIGHEST

SYSTEMS = 4
KRYLOV = 30
SEG = 128
ROWS = 16
COLS = 32
PANELS = SEG * ROWS * COLS
SOURCES = ROWS * SEG
CHUNK = 256
FEATURES = 128
CORE = 16.0 / PANELS
DEPTH = 16
PLANE = 32
NEAR = 8
REACH = 4
OUTWARD = (
    (2, 2), (2, 1), (2, 3), (1, 2), (3, 2), (1, 1), (1, 3), (3, 1),
    (3, 3), (2, 0), (0, 2), (1, 0), (3, 0), (0, 1), (0, 3), (0, 0),
)
EPSILON = 1e-06


def selections():
    source = np.zeros((FEATURES, 48), np.float32)
    target = np.zeros((FEATURES, 48), np.float32)
    coarse, fine, one = (0, 8), (16, 24), 38

    def products(at, lefts, rights):
        for left in lefts:
            for right in rights:
                for axis in range(3):
                    source[at, left + axis] = 1
                    target[at, right + axis] = -2
                    at += 1
        return at

    def norms(at, pieces):
        for piece in pieces:
            source[at, piece] = target[at, one] = 1
            source[at + 1, one] = target[at + 1, piece] = 1
            at += 2
        return at

    norms(products(0, coarse, coarse), (32, 33, 34))
    at = products(32, coarse, fine)
    at = products(at, fine, coarse + fine)
    norms(at, (35, 36, 37))
    return source, target


def rounded(a):
    return a.astype(bf16).astype(f32)


def pieces_of(points, extra):
    at = lax.broadcasted_iota(jnp.int32, (8, SEG), 0)
    points = jnp.where(at < 3, points, 0.0)
    coarse = jnp.floor(points * 128.0 + 0.5) * (1.0 / 128.0)
    fine = points - coarse
    coarse_high = rounded(coarse)
    fine_high = rounded(fine)
    fine_low = rounded(fine - fine_high)
    norm = jnp.sum(coarse * coarse, axis=0, keepdims=True)
    rest = jnp.sum(2.0 * coarse * fine + fine * fine, axis=0, keepdims=True) + extra
    tail = jnp.where(at == 6, 1.0, 0.0)
    row = 0
    for whole in (norm, rest):
        for _ in range(3):
            piece = rounded(whole)
            tail = jnp.where(at == row, piece, tail)
            whole = whole - piece
            row += 1
    rows = [coarse_high, coarse - coarse_high, fine_high, fine_low, tail, jnp.zeros((8, SEG), f32)]
    return jnp.concatenate(rows, axis=0).astype(bf16)


def contract(a, b, dims, **kw):
    return lax.dot_general(a, b, ((dims[:1], dims[1:]), ((), ())), preferred_element_type=f32, **kw)


def load_basis(basis,bmat):
    bmat[...]=jnp.zeros_like(bmat)
    for s in range(SYSTEMS):
        bmat[32*s:32*s+KRYLOV,:]=basis[s]
def two_sum(a,b):
    s=a+b
    t=s-a
    return s,(a-(s-t))+(b-t)
def pair_sum(p,q):
    s,e=two_sum(p[0],q[0])
    e=e+(p[1]+q[1])
    h=s+e
    return h,e-(h-s)
def pair_product(a,b):
    p=a*b
    ah,bh=rounded(a),rounded(b)
    al,bl=a-ah,b-bh
    return p,((ah*bh-p)+ah*bl+al*bh)+al*bl
def fold(parts):
    while len(parts)>1:
        parts=[pair_sum(*parts[i:i+2]) if i+1<len(parts) else parts[i] for i in range(0,len(parts),2)]
    return parts[0]
def down(p):
    m=p[0].shape[0]//8
    p=fold([(p[0][8*i:8*i+8],p[1][8*i:8*i+8]) for i in range(m)])
    for by in (4,2,1):
        p=pair_sum(p,(pltpu.roll(p[0],by,0),pltpu.roll(p[1],by,0)))
    return p[0][0:1],p[1][0:1]
def across(by_row):
    lane=lax.broadcasted_iota(jnp.int32,(32,SEG),1)//32
    out=by_row[0:32]
    for s in range(1,SYSTEMS):
        out=jnp.where(lane==s,by_row[32*s:32*s+32],out)
    return out
def gram(b):
    slices=[]
    rest=b
    for bits in (4,12,20,28):
        q=jnp.floor(rest*2.0**bits+0.5)*2.0**-bits
        rest=rest-q
        slices.append(q.astype(bf16))
    total=None
    for level in range(5):
        pairs=[(i,level-i) for i in range(4) if 0<=level-i<4]
        left=jnp.concatenate([slices[i] for i,_ in pairs],axis=1)
        right=jnp.concatenate([slices[j] for _,j in pairs],axis=1)
        part=across(contract(left,right,(1,1)))
        exact=(part,jnp.zeros_like(part))
        total=exact if total is None else pair_sum(total,exact)
    return total[0]*(1.0/PANELS),total[1]*(1.0/PANELS)
def payload(a,bt):
    lane=lax.broadcasted_iota(jnp.int32,(SEG,SEG),1)%32
    at=jnp.concatenate([jnp.broadcast_to(a[s:s+1],(32,SEG)) for s in range(SYSTEMS)],axis=0).T
    h,l=down(pair_product(at,jnp.where(lane==KRYLOV,at,bt)))
    return h*(1.0 / PANELS),l*(1.0 / PANELS)
def finish(a,p,g,bmat):
    k=lax.broadcasted_iota(jnp.int32,(1,SEG),1)%32
    system=lax.broadcasted_iota(jnp.int32,(8,SEG),0)
    lane=lax.broadcasted_iota(jnp.int32,(8,SEG),1)
    own=lane//32==system
    def times(c):
        column=across(jnp.broadcast_to(c,(SEG,SEG)).T)
        h,l=pair_product(g[0],column)
        return down((h,l+g[1]*column))
    basis_lane=k<KRYLOV
    fh,fl=jnp.where(basis_lane,p[0],0.0),jnp.where(basis_lane,p[1],0.0)
    gf=times(fh)
    second=(fh-gf[0])+(fl-gf[1])
    c=fh+second
    a8=jnp.concatenate([a,jnp.zeros((4,SEG),f32)],axis=0)
    twice=a8-contract(jnp.where(own,jnp.broadcast_to(c,(8,SEG)),0.0),bmat,(1,0),precision=HIGHEST)
    gc=times(c)
    u=pair_sum(gc,(-2.0*fh,-2.0*fl))
    h,l=pair_product(c,u[0])
    l=l+c*u[1]
    square=(jnp.where(k==KRYLOV,p[0],h),jnp.where(k==KRYLOV,p[1],l))
    for by in (1,2,4,8,16):
        square=pair_sum(square,(pltpu.roll(square[0],by,1),pltpu.roll(square[1],by,1)))
    length=jnp.sqrt(jnp.maximum(square[0]+square[1],0.0)+EPSILON)
    each=jnp.sum(jnp.where(own&(lane%32==31),jnp.broadcast_to(length,(8,SEG)),0.0),axis=1,keepdims=True)
    new=(twice/jnp.where(system[:,0:1]<SYSTEMS,each,1.0))[0:SYSTEMS]
    return new,jnp.where(k==KRYLOV,pltpu.roll(length,SEG-1,1),c)


def step_kernel(
    centroids, weight, basis, source_sel, target_sel, new_vector, hessenberg,
    src, tgt, feat, meet, vecs, sums, part, landed, bmat, bmat_t, gram_out, gram_in, gram_z, gram_all,
    dots_z, dots_q, send_sem, recv_sem,
):
    r, c = lax.axis_index("row"), lax.axis_index("col")
    z, q = c // 2, 2 * r + lax.rem(c, 2)

    def on_line(i):
        return r, lax.rem(c + 2 * i, 2 * DEPTH)

    def on_plane(to):
        return to // 2, 2 * z + lax.rem(to, 2)

    def near_offset(i):
        return lax.rem(DEPTH - REACH - 1 + i + lax.select(i > REACH, 1, 0), DEPTH)

    barrier = pltpu.get_barrier_semaphore()

    @pl.loop(1, 2 * REACH + 1)
    def _(i):
        pl.semaphore_signal(
            barrier, inc=1, device_id=on_line(near_offset(i)), device_id_type=MESH
        )

    @pl.loop(1, PLANE)
    def _(i):
        pl.semaphore_signal(
            barrier, inc=1, device_id=on_plane(lax.rem(q + i, PLANE)), device_id_type=MESH
        )

    def send(piece, place, sem, device):
        pltpu.make_async_remote_copy(
            src_ref=piece, dst_ref=place, send_sem=send_sem.at[sem], recv_sem=recv_sem.at[sem],
            device_id=device, device_id_type=MESH,
        ).start()

    def to_line(buf, sem):
        @pl.loop(1, DEPTH)
        def _(i):
            send(buf.at[z], buf.at[z], sem, on_line(i))

    def to_plane(buf, sem):
        @pl.loop(1, PLANE)
        def _(i):
            send(buf.at[q], buf.at[q], sem, on_plane(lax.rem(q + i, PLANE)))

    def settle(buf, count, sem):
        view = buf.at[pl.ds(0, count)]
        pltpu.make_async_copy(view, view, sem).wait()

    own_slot = 3
    src[own_slot, 0:3, :] = centroids[...]
    src[own_slot, 3:4, :] = weight[...]
    for s in range(SYSTEMS):
        src[own_slot, 4 + s : 5 + s, :] = basis[s, KRYLOV - 1 : KRYLOV, :]
    tgt[q, 0:3, :] = centroids[...]
    tgt[q, 3:4, :] = weight[...]

    pl.semaphore_wait(barrier, 2 * REACH + PLANE - 1)

    def to_slot(i, sem):
        send(src.at[own_slot], src.at[lax.rem(i + own_slot, DEPTH)], sem, on_line(i))

    @pl.loop(2, 2 * REACH + 1)
    def _(i):
        to_slot(near_offset(i), 0)

    to_plane(tgt, 2)
    to_slot(DEPTH - REACH, 1)

    load_basis(basis, bmat)
    bmat_t[...] = bmat[...].T
    gram_high, gram_low = gram(bmat[...])
    for k in range(PLANE):
        gram_out[k, 0:1, :] = gram_high[k : k + 1]
        gram_out[k, 1:2, :] = gram_low[k : k + 1]
    gram_in[q] = gram_out[q]

    @pl.loop(1, PLANE)
    def _(i):
        to = lax.rem(q + i, PLANE)
        send(gram_out.at[to], gram_in.at[q], 3, on_plane(to))

    def prepare(slots):
        for b in slots:
            block = src[b]
            pieces = pieces_of(block, block[3:4] * CORE)
            rows = slice(b * SEG, (b + 1) * SEG)
            feat[rows, :] = contract(pieces, source_sel[...], (0, 1)).astype(bf16)
            scaled = block[4:8] * (block[3:4] * (1.0 / PANELS**0.5))
            high = rounded(scaled)
            vecs[:, rows] = jnp.concatenate(
                [high, scaled - high, jnp.zeros((8, SEG), f32)], axis=0
            ).astype(bf16)

    def operate(meets, total, slots):
        for b in range(slots[0] // 2, slots[1] // 2):
            rows = slice(b * CHUNK, (b + 1) * CHUNK)
            entry = lax.rsqrt(contract(feat[rows, :], meets, (1, 0)))
            high = entry.astype(bf16)
            low = (entry - high.astype(f32)).astype(bf16)
            total = total + contract(vecs[:, rows], high, (1, 0))
            total = total + contract(vecs[:, rows], low, (1, 0))
        return total

    settle(src, NEAR - 1, recv_sem.at[0])
    ahead, behind = REACH, REACH - 1
    send(
        src.at[pl.ds(own_slot + 1, ahead)], src.at[pl.ds(own_slot + 1 + REACH, ahead)],
        1, on_line(REACH),
    )
    send(
        src.at[pl.ds(own_slot - behind, behind)],
        src.at[pl.ds(DEPTH - 1 - behind, behind)],
        1, on_line(DEPTH - REACH),
    )
    prepare(range(NEAR))
    settle(tgt, PLANE - 1, recv_sem.at[2])

    def other_chip(shift):
        return 4 * lax.rem(r // 4 + shift[0], 4) + lax.rem(lax.rem(r, 4) + shift[1], 4)

    def chosen(step, options):
        value = options[-1]
        for at in range(len(options) - 1):
            value = lax.select(step == at, options[at], value)
        return value

    for at in range(ROWS):
        other = other_chip(OUTWARD[at])
        pieces = []
        for core in range(2):
            block = jnp.concatenate([tgt[2 * other + core], jnp.zeros((4, SEG), f32)], axis=0)
            pieces.append(pieces_of(block, 0.0))
        pieces = jnp.concatenate(pieces, axis=1)
        meet[at] = contract(target_sel[...], pieces, (1, 0)).astype(bf16)

    nothing = jnp.zeros((16, CHUNK), f32)

    for at in range(ROWS - 1):
        sums[at] = operate(meet[at], nothing, (0, NEAR))

    def collect(buf, count):
        return fold([(buf[i, 0:1, :], buf[i, 1:2, :]) for i in range(count)])

    settle(src, DEPTH - NEAR, recv_sem.at[1])
    prepare(range(NEAR, DEPTH))

    def finished(at, other):
        total = operate(meet[at], sums[at], (NEAR, DEPTH))
        total = total[0:4] + total[4:8]
        part[2 * other] = total[:, 0:SEG]
        part[2 * other + 1] = total[:, SEG:CHUNK]

    def deliver(to):
        send(part.at[to], landed.at[q], 6, on_plane(to))

    for start in range(0, ROWS - 1, 8):
        others = [other_chip(shift) for shift in OUTWARD[start : min(start + 8, ROWS - 1)]]
        for i, other in enumerate(others):
            finished(start + i, other)
        for other in others:
            deliver(2 * other)
            deliver(2 * other + 1)

    sums[ROWS - 1] = operate(meet[ROWS - 1], nothing, (0, NEAR))
    finished(ROWS - 1, r)
    deliver(2 * r + 1 - lax.rem(c, 2))
    landed[q] = part[q]
    settle(gram_in, PLANE - 1, recv_sem.at[3])
    high, low = collect(gram_in, PLANE)
    gram_z[z, 0:1, :] = high
    gram_z[z, 1:2, :] = low
    to_line(gram_z, 4)

    settle(landed, PLANE - 1, recv_sem.at[6])
    applied = jnp.sum(landed[...], axis=0)

    high, low = payload(applied, bmat_t[...])
    dots_z[z, 0:1, :] = high
    dots_z[z, 1:2, :] = low
    to_line(dots_z, 7)
    settle(gram_z, DEPTH - 1, recv_sem.at[4])
    high, low = collect(gram_z, DEPTH)
    gram_all[q, 0:1, :] = high
    gram_all[q, 1:2, :] = low
    to_plane(gram_all, 5)
    settle(dots_z, DEPTH - 1, recv_sem.at[7])
    high, low = collect(dots_z, DEPTH)
    dots_q[q, 0:1, :] = high
    dots_q[q, 1:2, :] = low
    to_plane(dots_q, 8)
    settle(gram_all, PLANE - 1, recv_sem.at[5])
    gram_high = jnp.concatenate([gram_all[k, 0:1, :] for k in range(PLANE)], axis=0)
    gram_low = jnp.concatenate([gram_all[k, 1:2, :] for k in range(PLANE)], axis=0)
    settle(dots_q, PLANE - 1, recv_sem.at[8])
    vector, column = finish(applied, collect(dots_q, PLANE), (gram_high, gram_low), bmat[...])
    new_vector[...] = vector
    for s in range(SYSTEMS):
        hessenberg[s : s + 1, :] = column[:, 32 * s : 32 * s + KRYLOV + 1]

    settle(src, NEAR - 1, send_sem.at[0])
    settle(src, DEPTH - NEAR, send_sem.at[1])
    settle(tgt, PLANE - 1, send_sem.at[2])
    settle(gram_in, PLANE - 1, send_sem.at[3])
    settle(gram_z, DEPTH - 1, send_sem.at[4])
    settle(gram_all, PLANE - 1, send_sem.at[5])
    settle(landed, PLANE - 1, send_sem.at[6])
    settle(dots_z, DEPTH - 1, send_sem.at[7])
    settle(dots_q, PLANE - 1, send_sem.at[8])

def per_device(centroids, weight, basis):
    source, target = selections()
    vmem = pl.BlockSpec(memory_space=pltpu.VMEM)
    return pl.pallas_call(
        step_kernel,
        out_shape=(
            jax.ShapeDtypeStruct((SYSTEMS, SEG), f32),
            jax.ShapeDtypeStruct((SYSTEMS, KRYLOV + 1), f32),
        ),
        in_specs=[vmem] * 5,
        out_specs=(vmem, vmem),
        scratch_shapes=[
            pltpu.VMEM((DEPTH, 8, SEG), f32),
            pltpu.VMEM((PLANE, 4, SEG), f32),
            pltpu.VMEM((SOURCES, FEATURES), bf16),
            pltpu.VMEM((ROWS, FEATURES, CHUNK), bf16),
            pltpu.VMEM((16, SOURCES), bf16),
            pltpu.VMEM((ROWS, 16, CHUNK), f32),
            pltpu.VMEM((PLANE, 4, SEG), f32),
            pltpu.VMEM((PLANE, 4, SEG), f32),
            pltpu.VMEM((SEG, SEG), f32),
            pltpu.VMEM((SEG, SEG), f32),
            pltpu.VMEM((PLANE, 2, SEG), f32),
            pltpu.VMEM((PLANE, 2, SEG), f32),
            pltpu.VMEM((DEPTH, 2, SEG), f32),
            pltpu.VMEM((PLANE, 2, SEG), f32),
            pltpu.VMEM((DEPTH, 2, SEG), f32),
            pltpu.VMEM((PLANE, 2, SEG), f32),
            pltpu.SemaphoreType.DMA((9,)),
            pltpu.SemaphoreType.DMA((9,)),
        ],
        compiler_params=pltpu.CompilerParams(
            collective_id=0, has_side_effects=True, vmem_limit_bytes=40 * 2**20
        ),
        name="arnoldi_step",
    )(centroids, weight.reshape(1, SEG), basis, jnp.asarray(source, bf16), jnp.asarray(target, bf16))


def solution(mesh):
    placed = (P(None, ("col", "row")), P(("col", "row")), P(None, None, ("col", "row")))
    return jax.shard_map(
        per_device,
        mesh=mesh,
        in_specs=placed,
        out_specs=(P(None, ("col", "row")), P()),
        check_vma=False,
    )
```
